32 devices in a mesh: parts: 2 (over y), batch: 4 (over z), grp: 4 (over x, core).
Axes of the slice: x: 2, y: 2, z: 4, core: 2. Of those that a mesh axis runs over, the one named last changes fastest.
Arguments:
- queries: bfloat16 [8192, 2048], P(('parts', 'batch', 'grp')), parts along dimension 0, may hold values from -2 to 2
- passages: bfloat16 [4096, 2048], P(('parts', 'batch', 'grp')), parts along dimension 0, may hold values from -2 to 2
- hard_owners: int32 [8192, 2], P(('parts', 'batch', 'grp')), parts along dimension 0, may hold values from 0 to 3, all different within a row; in each aligned block of 256 rows (0 to 255, 256 to 511, ...) at most 170 rows name the same one
Outputs:
- query_loss: float32 [8192], P(('parts', 'batch', 'grp')), parts along dimension 0
- query_grad: bfloat16 [8192, 2048], P(('parts', 'batch', 'grp')), parts along dimension 0
- passage_grad: bfloat16 [4096, 2048], P(('parts', 'batch', 'grp')), parts along dimension 0
The draws below stay inside these ranges and needn't reach their ends.
There are 2 independent parts, one for each index of `parts`. The reference program is written for one: setup_inputs(seed, part) draws one part's arguments, and reference() takes and returns one part's arrays. A program takes and returns all parts, laid end to end along the dimension named above; each array names one. Nothing has to cross between parts.
Inputs may be any that keep to these rules, and one draw needn't show every extreme that they name: `hard_owners`: each row names 2 different batch indices. Among the 256 rows of one device no index is named more than 170 times, and on some devices some index is named exactly 170 times.
All inputs are finite; a program needn't handle non-finite values.
Results may differ from the reference program's by a relative error of at most 0.012.
Values may be sent and summed in bfloat16 or wider, within the bound.
A program may use at most 128 MiB of HBM per device.

```python
import math
import jax
import jax.numpy as jnp
import numpy as np
from jax import lax

D = 2048
QD = 256
PD = 128
K = 2
MOST = 170
QTOT = 4096
PTOT = 2048
N_BATCH = 4
N_GRP = 4


cluster_count = 8


def blend(key, row_count, col_count):
    normal_key = jax.random.fold_in(key, 0)
    gaussian = jax.random.truncated_normal(normal_key, -4.0, 4.0, (row_count, col_count), jnp.float32)
    return gaussian


def shared_parts(key):
    topic_key = jax.random.fold_in(key, 0)
    profile_key = jax.random.fold_in(key, 1)
    anchor_key = jax.random.fold_in(key, 3)
    topics = blend(topic_key, PTOT, D)
    profile = jax.random.uniform(profile_key, (1, D), jnp.float32, 0.6, 1.4)
    anchors = blend(anchor_key, N_GRP * PD, D)
    return (topics, profile, anchors)


def finish(key, values):
    row_key, col_key = jax.random.split(key)
    row_count, col_count = values.shape
    row_scale = jnp.exp(jax.random.uniform(row_key, (row_count, 1), jnp.float32, math.log(0.3), math.log(3.0)))
    col_scale = jnp.exp(jax.random.uniform(col_key, (1, col_count), jnp.float32, math.log(0.3), math.log(3.0)))
    mixed = values * row_scale * col_scale / (2.0 * math.sqrt(col_count))
    return jnp.clip(mixed, -2.0, 2.0).astype(jnp.bfloat16)


def draw_queries(key, part):
    topics, profile, anchors = shared_parts(key)
    key = jax.random.fold_in(key, 11)
    noise_key, factor_key, weight_key, scale_key, pick_key, anchor_weight_key = jax.random.split(key, 6)
    noise = blend(noise_key, QTOT, D)
    factors = jax.random.uniform(factor_key, (QTOT, cluster_count), jnp.float32, 0.5, 1.0)
    factor_wide = jnp.tile(factors, (1, D // cluster_count))
    topic_weight = jax.random.uniform(weight_key, (QTOT, 1), jnp.float32, 0.5, 2.0)
    row_ids = jnp.arange(QTOT, dtype=jnp.int32)
    positive = (row_ids // QD * PD + row_ids % QD % PD).astype(jnp.int32)
    anchor_pick = jax.random.randint(pick_key, (QTOT,), 0, PD, dtype=jnp.int32)
    anchor_rows = (row_ids // QD % N_GRP * PD + anchor_pick).astype(jnp.int32)
    anchor_weight = jax.random.uniform(anchor_weight_key, (QTOT, 1), jnp.float32, 1.0, 1.4)
    values = noise + factor_wide * profile + topic_weight * topics[positive] + anchor_weight * anchors[anchor_rows]
    return finish(scale_key, values)


def draw_passages(key, part):
    topics, profile, anchors = shared_parts(key)
    key = jax.random.fold_in(key, 23)
    noise_key, strength_key, scale_key, order_key, anchor_weight_key = jax.random.split(key, 5)
    noise = blend(noise_key, PTOT, D)
    strength = jax.random.uniform(strength_key, (PTOT, 1), jnp.float32, 0.5, 1.5)
    row_ids = jnp.arange(PTOT, dtype=jnp.int32)
    cluster = row_ids // (PD * N_GRP) % cluster_count
    member = ((jnp.arange(D, dtype=jnp.int32) % cluster_count)[None, :] == cluster[:, None]).astype(jnp.float32)
    block_keys = jax.random.split(order_key, N_BATCH * N_GRP)
    orders = jax.vmap(lambda block_key: jax.random.permutation(block_key, PD))(block_keys).reshape(-1).astype(jnp.int32)
    anchor_rows = (row_ids // PD % N_GRP * PD + orders).astype(jnp.int32)
    anchor_weight = jax.random.uniform(anchor_weight_key, (PTOT, 1), jnp.float32, 1.0, 1.4)
    values = noise + topics + 1.2 * math.sqrt(cluster_count) * strength * member * profile + anchor_weight * anchors[anchor_rows]
    return finish(scale_key, values)


def shared_out(key, own, number, rows, amount, top, bound, lean):
    order = jax.random.permutation(key, amount)
    packed, ordinary = shares(amount, rows * top, bound, lean, True), shares(amount, rows * top, bound, lean, False)
    places = jnp.arange(amount)

    def named(lengths, offset_by):
        used = int((lengths > 0).sum())
        fixed = max(1, used // 4)
        shifted = fixed + (places - fixed + offset_by * (used - fixed)) % max(1, amount - fixed)
        return jnp.zeros((amount,), jnp.int32).at[order[jnp.where(places < fixed, places, shifted)]].set(jnp.asarray(lengths, jnp.int32))

    lengths = jnp.where(number % 4 == 0, named(packed, number // 4), named(ordinary, number - number // 4 - 1))
    mixed = jax.random.permutation(jax.random.fold_in(own, 3), amount)
    donor, taker = mixed[0:amount // 2 * 2:2], mixed[1:amount // 2 * 2:2]
    margin = jnp.minimum(lengths[donor] - 1, bound - lengths[taker]) // 2
    margin = jnp.where((donor == order[0]) | (taker == order[0]) | (lengths[taker] == 0), 0, jnp.maximum(margin, 0))
    shifted = jax.random.randint(jax.random.fold_in(own, 4), (amount // 2,), 0, 1 << 20) % (margin + 1)
    lengths = lengths.at[donor].add(-shifted).at[taker].add(shifted)
    members = jnp.searchsorted(jnp.cumsum(lengths), jnp.arange(rows * top), side="right").astype(jnp.int32)
    listing = members.reshape(top, rows).T
    listing = listing[jax.random.permutation(jax.random.fold_in(own, 1), rows)]
    offset_by = jax.random.randint(jax.random.fold_in(own, 2), (rows, 1), 0, top)
    return jnp.take_along_axis(listing, (jnp.arange(top)[None, :] + offset_by) % top, axis=1)


def shares(amount, total, reach, slope, full):
    portions = [(1 << 20) // math.isqrt(grade ** slope) + 1 for grade in range(1, amount + 1)]
    largest = reach if full else min(reach, max(-(-total // amount), total * portions[0] // sum(portions)))
    least = 1 if total - largest >= amount - 1 else 0
    given, surplus = [largest] + [least] * (amount - 1), total - largest - least * (amount - 1)
    while surplus > 0:
        movable = [i for i in range(1, amount) if given[i] < largest] or [i for i in range(1, amount) if given[i] < reach]
        pool, remaining = sum([portions[i] for i in movable]), surplus
        for i in movable:
            extra = min(reach - given[i], max(1, remaining * portions[i] // pool), surplus)
            given[i] = given[i] + extra
            surplus = surplus - extra
    return np.array(given)


def setup_inputs(seed: int = 0, part: int = 0) -> dict:
    arg_keys = jax.random.split(jax.random.key(seed), 4)
    own_keys = jax.random.split(jax.random.fold_in(arg_keys[3], part), 4)
    queries = draw_queries(jax.random.fold_in(jax.random.fold_in(arg_keys[3], part), 71), part)
    passages = draw_passages(jax.random.fold_in(jax.random.fold_in(arg_keys[3], part), 71), part)
    hard_owners_keys = jax.random.split(jax.random.fold_in(own_keys[2], 1), QTOT // QD)
    hard_owners_turns = jax.random.permutation(jax.random.fold_in(own_keys[2], 3), QTOT // QD)
    hard_owners = jax.vmap(lambda own, number: shared_out(jax.random.fold_in(own_keys[2], 2), own, number, QD, N_BATCH, K, MOST, 2))(hard_owners_keys, hard_owners_turns).reshape((QTOT, K))
    return dict(queries=queries, passages=passages, hard_owners=hard_owners)


sharpness_factor = 20.0
norm_eps = 1e-06
peak_similarity = lax.Precision.HIGHEST

def unit_rows(embedded):
    widened = embedded.astype(jnp.float32)
    inverse_norm = lax.rsqrt(lax.optimization_barrier(jnp.sum(widened * widened, axis=-1, keepdims=True)) + norm_eps)
    return (widened * inverse_norm, inverse_norm)

def slot_layout(owner_table, owner_count, capacity):
    owner_list = owner_table.reshape(-1)
    onehot = (owner_list[:, None] == jnp.arange(owner_count, dtype=jnp.int32)[None, :]).astype(jnp.int32)
    before = jnp.cumsum(onehot, axis=0) - onehot
    rank_in_slot = lax.optimization_barrier(jnp.sum(before * onehot, axis=1))
    slot_place = (owner_list * capacity + rank_in_slot).astype(jnp.int32)
    pair_query = jnp.arange(owner_list.shape[0], dtype=jnp.int32) // owner_table.shape[1]
    holder = jnp.full((owner_count * capacity,), owner_table.shape[0], jnp.int32).at[slot_place].set(pair_query)
    return (slot_place, holder)

def back_project(unit, inverse_norm, direction):
    inner = lax.optimization_barrier(jnp.sum(unit * direction, axis=1, keepdims=True))
    return (inverse_norm * (direction - unit * inner)).astype(jnp.bfloat16)

def pick_rows(table, index):
    return jax.vmap(jax.vmap(lambda table_row, index_row: table_row[index_row]))(table, index)

def reference(queries, passages, hard_owners):
    query_unit, query_norm = unit_rows(queries)
    passage_unit, passage_norm = unit_rows(passages)
    query_half = lax.optimization_barrier(query_unit.astype(jnp.bfloat16))
    passage_half = lax.optimization_barrier(passage_unit.astype(jnp.bfloat16))
    query_grid = query_half.reshape(N_BATCH, N_GRP, QD, D)
    passage_grid = passage_half.reshape(N_BATCH, N_GRP, PD, D)
    owner_grid = hard_owners.reshape(N_BATCH, N_GRP, QD, K)
    layout = jax.vmap(jax.vmap(lambda owner_table: slot_layout(owner_table, N_BATCH, MOST)))
    slot_place, holder = layout(owner_grid)
    holder_grid = holder.reshape(N_BATCH, N_GRP, N_BATCH, MOST)
    padded_grid = jnp.concatenate([query_grid, jnp.zeros((N_BATCH, N_GRP, 1, D), jnp.bfloat16)], axis=2)

    def collected_operand(keeper_ordinal):
        seat_document_vectors = pick_rows(padded_grid, holder_grid[:, :, keeper_ordinal, :])
        return jnp.transpose(seat_document_vectors, (1, 0, 2, 3)).astype(jnp.float32)

    def owner_scores(keeper_ordinal):
        resident_tile_segment = passage_grid[keeper_ordinal].astype(jnp.float32)
        return sharpness_factor * jnp.einsum('lrhd,lbd->lrhb', collected_operand(keeper_ordinal), resident_tile_segment)
    owner_ids = jnp.arange(N_BATCH, dtype=jnp.int32)
    seat_similarity_values = lax.map(owner_scores, owner_ids)
    by_source = jnp.transpose(seat_similarity_values, (2, 1, 0, 3, 4)).reshape(N_BATCH, N_GRP, N_BATCH * MOST, PD)
    pair_scores = pick_rows(by_source, slot_place)
    hard_totals = lax.optimization_barrier(jnp.sum(jnp.exp(pair_scores).reshape(N_BATCH, N_GRP, QD, K * PD), axis=3))
    positive = jnp.arange(QD, dtype=jnp.int32) % PD
    column = jnp.arange(N_GRP, dtype=jnp.int32)[:, None] * PD + positive[None, :]
    matching_indicator = jnp.arange(N_GRP * PD, dtype=jnp.int32)[None, None, :] == column[:, :, None]

    def batch_row(batch_items):
        query_rows, passage_rows, totals_hard = batch_items
        document_vectors_by_team = passage_rows.reshape(N_GRP * PD, D).astype(jnp.float32)
        question_replicated = query_rows.astype(jnp.float32)
        entering_similarities = sharpness_factor * jnp.einsum('zct,ft->zcf', question_replicated, document_vectors_by_team)
        normalizer_logarithm = jnp.log(lax.optimization_barrier(jnp.sum(jnp.exp(entering_similarities), axis=2)) + totals_hard)
        query_loss = normalizer_logarithm - lax.optimization_barrier(jnp.sum(jnp.where(matching_indicator, entering_similarities, 0.0), axis=2))
        upstream_derivative = lax.optimization_barrier((sharpness_factor * (jnp.exp(entering_similarities - normalizer_logarithm[:, :, None]) - matching_indicator.astype(jnp.float32))).astype(jnp.bfloat16))
        grad_wide = upstream_derivative.astype(jnp.float32)
        query_in = jnp.einsum('gij,jd->gid', grad_wide, document_vectors_by_team)
        partials = lax.optimization_barrier(jnp.einsum('gij,gid->gjd', grad_wide, question_replicated).astype(jnp.bfloat16))
        passage_in = lax.optimization_barrier(jnp.sum(partials.astype(jnp.float32), axis=0)).reshape(N_GRP, PD, D)
        return (normalizer_logarithm, query_loss, query_in, passage_in)
    normalizer_logarithm, query_loss, query_in, passage_in = lax.map(batch_row, (query_grid, passage_grid, hard_totals))
    pair_weights = jnp.exp(pair_scores - jnp.repeat(normalizer_logarithm, K, axis=2)[..., None])
    fill_slots = jax.vmap(jax.vmap(lambda slot_index, weight_rows: jnp.zeros((N_BATCH * MOST, PD), jnp.float32).at[slot_index].set(weight_rows)))
    weight_slots = fill_slots(slot_place, pair_weights)
    weight_grid = jnp.transpose(weight_slots.reshape(N_BATCH, N_GRP, N_BATCH, MOST, PD), (2, 1, 0, 3, 4))
    group_ids = jnp.arange(N_GRP, dtype=jnp.int32)[:, None, None]
    batch_ids = jnp.arange(N_BATCH, dtype=jnp.int32)[None, :, None]

    def owner_step(accumulated, keeper_ordinal):
        seat_document_vectors = collected_operand(keeper_ordinal)
        normalized_share = weight_grid[keeper_ordinal]
        resident_tile_segment = passage_grid[keeper_ordinal].astype(jnp.float32)
        seat_backward_derivative = sharpness_factor * jnp.einsum('vsbf,vfi->vsbi', normalized_share, resident_tile_segment, precision=peak_similarity)
        midway_normalized_share = lax.optimization_barrier(normalized_share.astype(jnp.bfloat16)).astype(jnp.float32)
        hard_negative_documents = sharpness_factor * jnp.einsum('kudo,kudg->kog', midway_normalized_share, seat_document_vectors, precision=peak_similarity)
        slot_index = jnp.transpose(holder_grid[:, :, keeper_ordinal, :], (1, 0, 2))
        accumulated = accumulated.at[group_ids, batch_ids, slot_index].add(seat_backward_derivative)
        return (accumulated, hard_negative_documents)
    start_sum = jnp.zeros((N_GRP, N_BATCH, QD + 1, D), jnp.float32)
    hard_sum, hard_negative_documents = lax.scan(owner_step, start_sum, owner_ids)
    query_hard = jnp.transpose(hard_sum[:, :, :QD], (1, 0, 2, 3))
    query_dir = (query_in + query_hard).reshape(N_BATCH * N_GRP * QD, D)
    passage_dir = (passage_in + hard_negative_documents).reshape(N_BATCH * N_GRP * PD, D)
    return (query_loss.reshape(-1), back_project(query_unit, query_norm, query_dir), back_project(passage_unit, passage_norm, passage_dir))
```

```python
import jax
import jax.numpy as jnp
from jax import lax
from jax.sharding import PartitionSpec as P

sharpness_factor = 20.0
norm_eps = 1e-06


def shortened(value):

    def short(part):
        return part.astype(jnp.bfloat16) if part.dtype == jnp.float32 else part

    return jax.tree.map(short, value)


def unit_rows(embedded):
    widened = embedded.astype(jnp.float32)
    inverse_norm = lax.rsqrt(jnp.sum(widened * widened, axis=1, keepdims=True) + norm_eps)
    return (widened * inverse_norm, inverse_norm)


def slot_layout(owner_table, owner_count, capacity):
    owner_list = owner_table.reshape(-1)
    onehot = (owner_list[:, None] == jnp.arange(owner_count, dtype=jnp.int32)[None, :]).astype(
        jnp.int32
    )
    before = jnp.cumsum(onehot, axis=0) - onehot
    rank_in_slot = jnp.sum(before * onehot, axis=1)
    slot_place = owner_list * capacity + rank_in_slot
    pair_query = jnp.arange(owner_list.shape[0], dtype=jnp.int32) // owner_table.shape[1]
    holder = (
        jnp.full((owner_count * capacity,), owner_table.shape[0], jnp.int32)
        .at[slot_place]
        .set(pair_query)
    )
    return (slot_place, holder)


def back_project(unit, inverse_norm, direction):
    inner = jnp.sum(unit * direction, axis=1, keepdims=True)
    return (inverse_norm * (direction - unit * inner)).astype(jnp.bfloat16)


def local_slots(queries, passages, hard_owners):
    query_unit, query_norm = unit_rows(queries)
    passage_unit, passage_norm = unit_rows(passages)
    query_half = query_unit.astype(jnp.bfloat16)
    passage_half = passage_unit.astype(jnp.bfloat16)
    query_rows, embed_width = queries.shape
    passage_rows = passages.shape[0]
    picks_each = hard_owners.shape[1]
    batch_count = lax.axis_size("batch")
    group_count = lax.axis_size("grp")
    capacity = max(2, min(query_rows, 4 * query_rows * picks_each // (3 * batch_count)))
    slot_place, holder = slot_layout(hard_owners, batch_count, capacity)
    padded_queries = jnp.concatenate(
        [query_half, jnp.zeros((1, embed_width), jnp.bfloat16)], axis=0
    )
    outgoing = padded_queries[holder].reshape(batch_count, capacity, embed_width)
    arrived = lax.all_to_all(outgoing, "batch", split_axis=0, concat_axis=0, tiled=True).reshape(
        batch_count * capacity, embed_width
    )
    seat_similarity_values = sharpness_factor * jnp.einsum(
        "md,cd->mc", arrived, passage_half, preferred_element_type=jnp.float32
    )
    passage_wide = passage_half.astype(jnp.float32)
    document_vectors_by_team = lax.all_gather(passage_half, "grp", axis=0, tiled=True)
    entering_similarities = sharpness_factor * jnp.einsum(
        "id,jd->ij", query_half, document_vectors_by_team, preferred_element_type=jnp.float32
    )
    column = (
        lax.axis_index("grp") * passage_rows
        + jnp.arange(query_rows, dtype=jnp.int32) % passage_rows
    )
    matching_indicator = (
        jnp.arange(group_count * passage_rows, dtype=jnp.int32)[None, :] == column[:, None]
    )
    totals_in = jnp.sum(jnp.exp(entering_similarities), axis=1)
    returned = lax.all_to_all(
        seat_similarity_values.reshape(batch_count, capacity, passage_rows).astype(jnp.bfloat16),
        "batch",
        split_axis=0,
        concat_axis=0,
        tiled=True,
    ).astype(jnp.float32)
    pair_scores = returned.reshape(batch_count * capacity, passage_rows)[slot_place]
    totals = totals_in + jnp.sum(
        jnp.exp(pair_scores).reshape(query_rows, picks_each * passage_rows), axis=1
    )
    normalizer_logarithm = jnp.log(totals)
    pair_weights = jnp.exp(pair_scores - jnp.repeat(normalizer_logarithm, picks_each)[:, None])
    weight_slots = (
        jnp.zeros((batch_count * capacity, passage_rows), jnp.float32)
        .at[slot_place]
        .set(pair_weights)
    )
    slot_weights = (
        lax.all_to_all(
            weight_slots.reshape(batch_count, capacity, passage_rows).astype(jnp.bfloat16),
            "batch",
            split_axis=0,
            concat_axis=0,
            tiled=True,
        )
        .astype(jnp.float32)
        .reshape(batch_count * capacity, passage_rows)
    )
    seat_backward_derivative = sharpness_factor * jnp.dot(
        slot_weights, passage_wide, precision=lax.Precision.HIGHEST
    )
    home_rows = lax.all_to_all(
        shortened(seat_backward_derivative.reshape(batch_count, capacity, embed_width)),
        "batch",
        split_axis=0,
        concat_axis=0,
        tiled=True,
    )
    pair_rows = home_rows.reshape(batch_count * capacity, embed_width)[slot_place]
    hard_dir = jnp.sum(pair_rows.reshape(query_rows, picks_each, embed_width), axis=1)
    hard_negative_documents = sharpness_factor * jnp.einsum(
        "mc,md->cd", slot_weights.astype(jnp.bfloat16), arrived, preferred_element_type=jnp.float32
    )
    query_loss = normalizer_logarithm - jnp.sum(
        jnp.where(matching_indicator, entering_similarities, 0.0), axis=1
    )
    upstream_derivative = (
        sharpness_factor
        * (
            jnp.exp(entering_similarities - normalizer_logarithm[:, None])
            - matching_indicator.astype(jnp.float32)
        )
    ).astype(jnp.bfloat16)
    query_dir = (
        jnp.dot(upstream_derivative, document_vectors_by_team, preferred_element_type=jnp.float32)
        + hard_dir
    )
    passage_dir = (
        lax.psum_scatter(
            jnp.einsum(
                "ij,id->jd", upstream_derivative, query_half, preferred_element_type=jnp.float32
            ).astype(jnp.bfloat16),
            "grp",
            scatter_dimension=0,
            tiled=True,
        ).astype(jnp.float32)
        + hard_negative_documents
    )
    return (
        query_loss,
        back_project(query_unit, query_norm, query_dir),
        back_project(passage_unit, passage_norm, passage_dir),
    )


def local_dense(queries, passages, hard_owners):
    query_unit, query_norm = unit_rows(queries)
    passage_unit, passage_norm = unit_rows(passages)
    query_half = query_unit.astype(jnp.bfloat16)
    passage_half = passage_unit.astype(jnp.bfloat16)
    query_rows = queries.shape[0]
    passage_rows = passages.shape[0]
    batch_count = lax.axis_size("batch")
    group_count = lax.axis_size("grp")
    group_blocks = lax.all_gather(passage_half, "grp", axis=0, tiled=True)
    line_blocks = lax.all_gather(passage_half, "batch", axis=0, tiled=True)
    scores_in = sharpness_factor * jnp.einsum(
        "id,jd->ij", query_half, group_blocks, preferred_element_type=jnp.float32
    )
    scores_hard = sharpness_factor * jnp.einsum(
        "id,jd->ij", query_half, line_blocks, preferred_element_type=jnp.float32
    )
    block = jnp.arange(batch_count * passage_rows, dtype=jnp.int32)[None, :] // passage_rows
    named = jnp.any(hard_owners[:, :, None] == block[:, None, :], axis=1)
    column = (
        lax.axis_index("grp") * passage_rows
        + jnp.arange(query_rows, dtype=jnp.int32) % passage_rows
    )
    positive = (
        jnp.arange(group_count * passage_rows, dtype=jnp.int32)[None, :] == column[:, None]
    )
    raised_in = jnp.exp(scores_in)
    raised_hard = jnp.where(named, jnp.exp(scores_hard), 0.0)
    totals = jnp.sum(raised_in, axis=1) + jnp.sum(raised_hard, axis=1)
    log_total = jnp.log(totals)
    query_loss = log_total - jnp.sum(jnp.where(positive, scores_in, 0.0), axis=1)
    scale = sharpness_factor / totals
    grad_in = (
        raised_in * scale[:, None] - jnp.where(positive, sharpness_factor, 0.0)
    ).astype(jnp.bfloat16)
    grad_hard = (raised_hard * scale[:, None]).astype(jnp.bfloat16)
    query_dir = jnp.dot(
        grad_in, group_blocks, preferred_element_type=jnp.float32
    ) + jnp.dot(grad_hard, line_blocks, preferred_element_type=jnp.float32)

    def summed(grad, axis):
        partial = jnp.einsum("ij,id->jd", grad, query_half, preferred_element_type=jnp.float32)
        return lax.psum_scatter(
            partial.astype(jnp.bfloat16), axis, scatter_dimension=0, tiled=True
        ).astype(jnp.float32)

    passage_dir = summed(grad_in, "grp") + summed(grad_hard, "batch")
    return (
        query_loss,
        back_project(query_unit, query_norm, query_dir),
        back_project(passage_unit, passage_norm, passage_dir),
    )


def local(queries, passages, hard_owners):
    if lax.axis_size("batch") <= 8:
        return local_dense(queries, passages, hard_owners)
    return local_slots(queries, passages, hard_owners)


def solution(mesh):
    placed = (
        P(("parts", "batch", "grp"), None),
        P(("parts", "batch", "grp"), None),
        P(("parts", "batch", "grp"), None),
    )
    return jax.shard_map(
        local,
        mesh=mesh,
        in_specs=placed,
        out_specs=(
            P(("parts", "batch", "grp")),
            P(("parts", "batch", "grp"), None),
            P(("parts", "batch", "grp"), None),
        ),
        check_vma=False,
    )
```

```python
import functools

import jax
import jax.numpy as jnp
from jax import lax
from jax.experimental import pallas as pl
from jax.experimental.pallas import tpu as pltpu
from jax.sharding import PartitionSpec as P

sharpness_factor = 20.0
norm_eps = 1e-06


def shortened(value):

    def short(part):
        return part.astype(jnp.bfloat16) if part.dtype == jnp.float32 else part

    return jax.tree.map(short, value)


def unit_rows(embedded):
    widened = embedded.astype(jnp.float32)
    inverse_norm = lax.rsqrt(jnp.sum(widened * widened, axis=1, keepdims=True) + norm_eps)
    return (widened * inverse_norm, inverse_norm)


def slot_layout(owner_table, owner_count, capacity):
    owner_list = owner_table.reshape(-1)
    onehot = (owner_list[:, None] == jnp.arange(owner_count, dtype=jnp.int32)[None, :]).astype(
        jnp.int32
    )
    before = jnp.cumsum(onehot, axis=0) - onehot
    rank_in_slot = jnp.sum(before * onehot, axis=1)
    slot_place = owner_list * capacity + rank_in_slot
    pair_query = jnp.arange(owner_list.shape[0], dtype=jnp.int32) // owner_table.shape[1]
    holder = (
        jnp.full((owner_count * capacity,), owner_table.shape[0], jnp.int32)
        .at[slot_place]
        .set(pair_query)
    )
    return (slot_place, holder)


def back_project(unit, inverse_norm, direction):
    inner = jnp.sum(unit * direction, axis=1, keepdims=True)
    return (inverse_norm * (direction - unit * inner)).astype(jnp.bfloat16)


def local_slots(queries, passages, hard_owners):
    query_unit, query_norm = unit_rows(queries)
    passage_unit, passage_norm = unit_rows(passages)
    query_half = query_unit.astype(jnp.bfloat16)
    passage_half = passage_unit.astype(jnp.bfloat16)
    query_rows, embed_width = queries.shape
    passage_rows = passages.shape[0]
    picks_each = hard_owners.shape[1]
    batch_count = lax.axis_size("batch")
    group_count = lax.axis_size("grp")
    capacity = max(2, min(query_rows, 4 * query_rows * picks_each // (3 * batch_count)))
    slot_place, holder = slot_layout(hard_owners, batch_count, capacity)
    padded_queries = jnp.concatenate(
        [query_half, jnp.zeros((1, embed_width), jnp.bfloat16)], axis=0
    )
    outgoing = padded_queries[holder].reshape(batch_count, capacity, embed_width)
    arrived = lax.all_to_all(outgoing, "batch", split_axis=0, concat_axis=0, tiled=True).reshape(
        batch_count * capacity, embed_width
    )
    seat_similarity_values = sharpness_factor * jnp.einsum(
        "md,cd->mc", arrived, passage_half, preferred_element_type=jnp.float32
    )
    passage_wide = passage_half.astype(jnp.float32)
    document_vectors_by_team = lax.all_gather(passage_half, "grp", axis=0, tiled=True)
    entering_similarities = sharpness_factor * jnp.einsum(
        "id,jd->ij", query_half, document_vectors_by_team, preferred_element_type=jnp.float32
    )
    column = (
        lax.axis_index("grp") * passage_rows
        + jnp.arange(query_rows, dtype=jnp.int32) % passage_rows
    )
    matching_indicator = (
        jnp.arange(group_count * passage_rows, dtype=jnp.int32)[None, :] == column[:, None]
    )
    totals_in = jnp.sum(jnp.exp(entering_similarities), axis=1)
    returned = lax.all_to_all(
        seat_similarity_values.reshape(batch_count, capacity, passage_rows).astype(jnp.bfloat16),
        "batch",
        split_axis=0,
        concat_axis=0,
        tiled=True,
    ).astype(jnp.float32)
    pair_scores = returned.reshape(batch_count * capacity, passage_rows)[slot_place]
    totals = totals_in + jnp.sum(
        jnp.exp(pair_scores).reshape(query_rows, picks_each * passage_rows), axis=1
    )
    normalizer_logarithm = jnp.log(totals)
    pair_weights = jnp.exp(pair_scores - jnp.repeat(normalizer_logarithm, picks_each)[:, None])
    weight_slots = (
        jnp.zeros((batch_count * capacity, passage_rows), jnp.float32)
        .at[slot_place]
        .set(pair_weights)
    )
    slot_weights = (
        lax.all_to_all(
            weight_slots.reshape(batch_count, capacity, passage_rows).astype(jnp.bfloat16),
            "batch",
            split_axis=0,
            concat_axis=0,
            tiled=True,
        )
        .astype(jnp.float32)
        .reshape(batch_count * capacity, passage_rows)
    )
    seat_backward_derivative = sharpness_factor * jnp.dot(
        slot_weights, passage_wide, precision=lax.Precision.HIGHEST
    )
    home_rows = lax.all_to_all(
        shortened(seat_backward_derivative.reshape(batch_count, capacity, embed_width)),
        "batch",
        split_axis=0,
        concat_axis=0,
        tiled=True,
    )
    pair_rows = home_rows.reshape(batch_count * capacity, embed_width)[slot_place]
    hard_dir = jnp.sum(pair_rows.reshape(query_rows, picks_each, embed_width), axis=1)
    hard_negative_documents = sharpness_factor * jnp.einsum(
        "mc,md->cd", slot_weights.astype(jnp.bfloat16), arrived, preferred_element_type=jnp.float32
    )
    query_loss = normalizer_logarithm - jnp.sum(
        jnp.where(matching_indicator, entering_similarities, 0.0), axis=1
    )
    upstream_derivative = (
        sharpness_factor
        * (
            jnp.exp(entering_similarities - normalizer_logarithm[:, None])
            - matching_indicator.astype(jnp.float32)
        )
    ).astype(jnp.bfloat16)
    query_dir = (
        jnp.dot(upstream_derivative, document_vectors_by_team, preferred_element_type=jnp.float32)
        + hard_dir
    )
    passage_dir = (
        lax.psum_scatter(
            jnp.einsum(
                "ij,id->jd", upstream_derivative, query_half, preferred_element_type=jnp.float32
            ).astype(jnp.bfloat16),
            "grp",
            scatter_dimension=0,
            tiled=True,
        ).astype(jnp.float32)
        + hard_negative_documents
    )
    return (
        query_loss,
        back_project(query_unit, query_norm, query_dir),
        back_project(passage_unit, passage_norm, passage_dir),
    )


def local_dense(queries, passages, hard_owners):
    query_unit, query_norm = unit_rows(queries)
    passage_unit, passage_norm = unit_rows(passages)
    query_half = query_unit.astype(jnp.bfloat16)
    passage_half = passage_unit.astype(jnp.bfloat16)
    query_rows = queries.shape[0]
    passage_rows = passages.shape[0]
    batch_count = lax.axis_size("batch")
    group_count = lax.axis_size("grp")
    group_blocks = lax.all_gather(passage_half, "grp", axis=0, tiled=True)
    line_blocks = lax.all_gather(passage_half, "batch", axis=0, tiled=True)
    scores_in = sharpness_factor * jnp.einsum(
        "id,jd->ij", query_half, group_blocks, preferred_element_type=jnp.float32
    )
    scores_hard = sharpness_factor * jnp.einsum(
        "id,jd->ij", query_half, line_blocks, preferred_element_type=jnp.float32
    )
    block = jnp.arange(batch_count * passage_rows, dtype=jnp.int32)[None, :] // passage_rows
    named = jnp.any(hard_owners[:, :, None] == block[:, None, :], axis=1)
    column = (
        lax.axis_index("grp") * passage_rows
        + jnp.arange(query_rows, dtype=jnp.int32) % passage_rows
    )
    positive = (
        jnp.arange(group_count * passage_rows, dtype=jnp.int32)[None, :] == column[:, None]
    )
    raised_in = jnp.exp(scores_in)
    raised_hard = jnp.where(named, jnp.exp(scores_hard), 0.0)
    totals = jnp.sum(raised_in, axis=1) + jnp.sum(raised_hard, axis=1)
    log_total = jnp.log(totals)
    query_loss = log_total - jnp.sum(jnp.where(positive, scores_in, 0.0), axis=1)
    scale = sharpness_factor / totals
    grad_in = (
        raised_in * scale[:, None] - jnp.where(positive, sharpness_factor, 0.0)
    ).astype(jnp.bfloat16)
    grad_hard = (raised_hard * scale[:, None]).astype(jnp.bfloat16)
    query_dir = jnp.dot(
        grad_in, group_blocks, preferred_element_type=jnp.float32
    ) + jnp.dot(grad_hard, line_blocks, preferred_element_type=jnp.float32)

    def summed(grad, axis):
        partial = jnp.einsum("ij,id->jd", grad, query_half, preferred_element_type=jnp.float32)
        return lax.psum_scatter(
            partial.astype(jnp.bfloat16), axis, scatter_dimension=0, tiled=True
        ).astype(jnp.float32)

    passage_dir = summed(grad_in, "grp") + summed(grad_hard, "batch")
    return (
        query_loss,
        back_project(query_unit, query_norm, query_dir),
        back_project(passage_unit, passage_norm, passage_dir),
    )


CHUNKS = 2
ROWS = 32
MESH = pl.DeviceIdType.MESH


def dot(left, right, left_dim, right_dim):
    return lax.dot_general(
        left,
        right,
        (((left_dim,), (right_dim,)), ((), ())),
        preferred_element_type=jnp.float32,
    )


def fused_kernel(
    nb, ng,
    queries, passages, owners,
    loss_out, query_out, passage_out,
    line, group, query_half, query_norm, passage_norm,
    grad_in, grad_hard, query_dir,
    hard_sums, from_left, from_right, in_sums, from_group,
    gather_send, gather_recv, group_send, group_recv,
    reduce_send, reduce_recv, back_send, back_recv,
):
    b = lax.axis_index("batch")
    g = lax.axis_index("grp")
    rows, width = queries.shape
    block = passages.shape[0]
    part = block // CHUNKS
    last = nb - 1

    def when(condition, act):
        pl.when(condition)(act)

    def piece(c):
        return pl.ds(c * part, part)

    def along(src, dst, send, recv, step):
        return pltpu.make_async_remote_copy(
            src_ref=src, dst_ref=dst, send_sem=send, recv_sem=recv,
            device_id={"batch": b + step}, device_id_type=MESH,
        )

    def gather(way, owner, s, c):
        ref = line.at[owner, piece(c)]
        return along(ref, ref, gather_send.at[way, s, c], gather_recv.at[way, s, c], 1 - 2 * way)

    def group_copy(src, dst, send, recv, k):
        return pltpu.make_async_remote_copy(
            src_ref=src, dst_ref=dst, send_sem=send.at[k], recv_sem=recv.at[k],
            device_id={"grp": lax.rem(g + k, ng)}, device_id_type=MESH,
        )

    def reduce(way, s, c):
        target = s if way else last - s
        landing = from_right if way else from_left
        return along(
            hard_sums.at[target, piece(c)], landing.at[s, piece(c)],
            reduce_send.at[way, s, c], reduce_recv.at[way, s, c], 1 - 2 * way,
        )

    barrier = pltpu.get_barrier_semaphore()

    def greet(step):
        pl.semaphore_signal(
            barrier, inc=1, device_id={"batch": b + step}, device_id_type=MESH
        )

    when(b > 0, lambda: greet(-1))
    when(b < last, lambda: greet(1))
    for k in range(1, ng):
        pl.semaphore_signal(
            barrier, inc=1, device_id={"grp": lax.rem(g + k, ng)}, device_id_type=MESH
        )

    def norm_passages(i, _):
        at = pl.ds(pl.multiple_of(i * ROWS, ROWS), ROWS)
        wide = passages[at, :].astype(jnp.float32)
        norm = lax.rsqrt(jnp.sum(wide * wide, axis=1, keepdims=True) + norm_eps)
        half = (wide * norm).astype(jnp.bfloat16)
        passage_norm[at, :] = norm
        line[b, at, :] = half
        group[g, at, :] = half
        return _

    lax.fori_loop(0, block // ROWS, norm_passages, 0)
    pl.semaphore_wait(
        barrier, ng - 1 + (b > 0).astype(jnp.int32) + (b < last).astype(jnp.int32)
    )
    for c in range(CHUNKS):
        when(b < last, lambda: gather(0, b, 0, c).start())
        when(b > 0, lambda: gather(1, b, 0, c).start())
    for k in range(1, ng):
        group_copy(group.at[g], group.at[g], group_send, group_recv, k).start()

    def norm_queries(i, _):
        at = pl.ds(pl.multiple_of(i * ROWS, ROWS), ROWS)
        wide = queries[at, :].astype(jnp.float32)
        norm = lax.rsqrt(jnp.sum(wide * wide, axis=1, keepdims=True) + norm_eps)
        query_norm[at, :] = norm
        query_half[at, :] = (wide * norm).astype(jnp.bfloat16)
        return _

    lax.fori_loop(0, rows // ROWS, norm_queries, 0)

    def take(way, s, c):
        owner = b + 1 + s if way else b - 1 - s

        def pass_on():
            gather(way, owner, s + 1, c).start()

        def arrive():
            gather(way, owner, s, c).wait_recv()
            if s + 1 < last:
                when(b > 0 if way else b < last, pass_on)

        when(owner <= last if way else owner >= 0, arrive)

    for s in range(last):
        for c in range(CHUNKS):
            take(0, s, c)
            take(1, s, c)
    for k in range(1, ng):
        source = lax.rem(g + ng - k, ng)
        group_copy(
            group.at[source], group.at[source], group_send, group_recv, k
        ).wait_recv()

    units = query_half[...]
    scores_in = sharpness_factor * dot(
        units, group[...].reshape(ng * block, width), 1, 1
    )
    scores_hard = sharpness_factor * dot(
        units, line[...].reshape(nb * block, width), 1, 1
    )
    raised_in = jnp.exp(scores_in)
    names = owners[...]
    raised_hard = []
    for n in range(nb):
        named = jnp.any(names == n, axis=1, keepdims=True)
        raised_hard.append(
            jnp.where(named, jnp.exp(scores_hard[:, n * block:(n + 1) * block]), 0.0)
        )
    totals = jnp.sum(raised_in, axis=1, keepdims=True) + jnp.sum(
        functools.reduce(jnp.add, raised_hard), axis=1, keepdims=True
    )
    shape = (rows, ng * block)
    column = g * block + lax.rem(lax.broadcasted_iota(jnp.int32, shape, 0), block)
    positive = lax.broadcasted_iota(jnp.int32, shape, 1) == column
    losses = jnp.log(totals) - jnp.sum(
        jnp.where(positive, scores_in, 0.0), axis=1, keepdims=True
    )
    square = (block, block)
    diagonal = lax.broadcasted_iota(jnp.int32, square, 0) == lax.broadcasted_iota(
        jnp.int32, square, 1
    )
    for i in range(rows // block):
        loss_out[i:i + 1, :] = jnp.sum(
            jnp.where(diagonal, losses[i * block:(i + 1) * block], 0.0), axis=0, keepdims=True
        )
    scale = sharpness_factor / totals
    for n in range(nb):
        grad_hard[:, n * block:(n + 1) * block] = (raised_hard[n] * scale).astype(jnp.bfloat16)
    grad_in[...] = (
        raised_in * scale - jnp.where(positive, sharpness_factor, 0.0)
    ).astype(jnp.bfloat16)

    for n in sorted(range(nb), key=lambda n: -abs(2 * n - last)):
        hard_sums[n] = dot(
            grad_hard[:, n * block:(n + 1) * block], query_half[...], 0, 0
        ).astype(jnp.bfloat16)
        for c in range(CHUNKS):
            if n > 0:
                when(b == 0, lambda: reduce(0, last - n, c).start())
            if n < last:
                when(b == last, lambda: reduce(1, n, c).start())
    for h in range(ng):
        in_sums[h] = dot(
            grad_in[:, h * block:(h + 1) * block], query_half[...], 0, 0
        ).astype(jnp.bfloat16)

    def back_copy(k):
        return group_copy(
            in_sums.at[lax.rem(g + k, ng)], from_group.at[k - 1], back_send, back_recv, k
        )

    for k in range(1, ng):
        back_copy(k).start()

    tile = min(512, width)
    for j in range(0, width, tile):
        query_dir[:, j:j + tile] = dot(
            grad_in[...], group[:, :, j:j + tile].reshape(ng * block, tile), 1, 0
        ) + dot(grad_hard[...], line[:, :, j:j + tile].reshape(nb * block, tile), 1, 0)

    def finish_queries(i, _):
        at = pl.ds(pl.multiple_of(i * ROWS, ROWS), ROWS)
        norm = query_norm[at, :]
        unit = queries[at, :].astype(jnp.float32) * norm
        direction = query_dir[at, :]
        inner = jnp.sum(unit * direction, axis=1, keepdims=True)
        query_out[at, :] = (norm * (direction - unit * inner)).astype(jnp.bfloat16)
        return _

    lax.fori_loop(0, rows // ROWS, finish_queries, 0)

    def add_and_pass(way, s, c):
        target = s if way else last - s
        landing = from_right if way else from_left

        def act():
            reduce(way, s, c).wait_recv()
            own = hard_sums[target, piece(c), :].astype(jnp.float32)
            hard_sums[target, piece(c), :] = (
                own + landing[s, piece(c), :].astype(jnp.float32)
            ).astype(jnp.bfloat16)
            reduce(way, s, c).start()

        when((b < last) & (b > target) if way else (b > 0) & (b < target), act)

    for s in range(last):
        for c in range(CHUNKS):
            add_and_pass(0, s, c)
            add_and_pass(1, s, c)
    for k in range(1, ng):
        back_copy(k).wait_recv()

    def finish_passages(at):
        total = hard_sums[b, at, :].astype(jnp.float32) + in_sums[g, at, :].astype(jnp.float32)
        for k in range(ng - 1):
            total += from_group[k, at, :].astype(jnp.float32)
        return total

    left_at = jnp.minimum(last - b, last - 1)
    right_at = jnp.minimum(b, last - 1)
    for c in range(CHUNKS):
        for way in (0, 1):
            for s in range(last):
                target = s if way else last - s
                when(b == target, lambda: reduce(way, s, c).wait_recv())

        def finish(i, _):
            at = pl.ds(pl.multiple_of(c * part + i * ROWS, ROWS), ROWS)
            direction = finish_passages(at)
            direction += jnp.where(b > 0, from_left[left_at, at, :].astype(jnp.float32), 0.0)
            direction += jnp.where(b < last, from_right[right_at, at, :].astype(jnp.float32), 0.0)
            norm = passage_norm[at, :]
            unit = passages[at, :].astype(jnp.float32) * norm
            inner = jnp.sum(unit * direction, axis=1, keepdims=True)
            passage_out[at, :] = (norm * (direction - unit * inner)).astype(jnp.bfloat16)
            return _

        lax.fori_loop(0, part // ROWS, finish, 0)

    for s in range(last):
        for c in range(CHUNKS):
            when((b < last) & (b >= s), lambda: gather(0, b - s, s, c).wait_send())
            when((b > 0) & (b + s <= last), lambda: gather(1, b + s, s, c).wait_send())
            when(b < last - s, lambda: reduce(0, s, c).wait_send())
            when(b > s, lambda: reduce(1, s, c).wait_send())
    for k in range(1, ng):
        group_copy(group.at[g], group.at[g], group_send, group_recv, k).wait_send()
        back_copy(k).wait_send()


def local_fused(queries, passages, hard_owners):
    rows, width = queries.shape
    block = passages.shape[0]
    nb, ng = lax.axis_size("batch"), lax.axis_size("grp")
    half, wide = jnp.bfloat16, jnp.float32
    vmem = pl.BlockSpec(memory_space=pltpu.VMEM)
    line_sems = pltpu.SemaphoreType.DMA((2, nb - 1, CHUNKS))
    group_sems = pltpu.SemaphoreType.DMA((ng,))
    loss, query_grad, passage_grad = pl.pallas_call(
        functools.partial(fused_kernel, nb, ng),
        out_shape=(
            jax.ShapeDtypeStruct((rows // block, block), wide),
            jax.ShapeDtypeStruct((rows, width), half),
            jax.ShapeDtypeStruct((block, width), half),
        ),
        in_specs=[vmem] * 3,
        out_specs=(vmem,) * 3,
        scratch_shapes=[
            pltpu.VMEM((nb, block, width), half),
            pltpu.VMEM((ng, block, width), half),
            pltpu.VMEM((rows, width), half),
            pltpu.VMEM((rows, 1), wide),
            pltpu.VMEM((block, 1), wide),
            pltpu.VMEM((rows, ng * block), half),
            pltpu.VMEM((rows, nb * block), half),
            pltpu.VMEM((rows, width), wide),
            pltpu.VMEM((nb, block, width), half),
            pltpu.VMEM((nb - 1, block, width), half),
            pltpu.VMEM((nb - 1, block, width), half),
            pltpu.VMEM((ng, block, width), half),
            pltpu.VMEM((ng - 1, block, width), half),
            line_sems, line_sems, group_sems, group_sems,
            line_sems, line_sems, group_sems, group_sems,
        ],
        compiler_params=pltpu.CompilerParams(
            collective_id=0, has_side_effects=True, vmem_limit_bytes=48 * 1024 * 1024
        ),
        cost_estimate=pl.CostEstimate(
            flops=6 * rows * (nb + ng) * block * width,
            bytes_accessed=4 * (rows + block) * width,
            transcendentals=rows * (nb + ng) * block,
        ),
    )(queries, passages, hard_owners)
    return (loss.reshape(-1), query_grad, passage_grad)


def local(queries, passages, hard_owners):
    nb = lax.axis_size("batch")
    if 1 < nb <= 8 and 1 < lax.axis_size("grp") <= 8:
        return local_fused(queries, passages, hard_owners)
    if nb <= 8:
        return local_dense(queries, passages, hard_owners)
    return local_slots(queries, passages, hard_owners)


def solution(mesh):
    placed = (
        P(("parts", "batch", "grp"), None),
        P(("parts", "batch", "grp"), None),
        P(("parts", "batch", "grp"), None),
    )
    return jax.shard_map(
        local,
        mesh=mesh,
        in_specs=placed,
        out_specs=(
            P(("parts", "batch", "grp")),
            P(("parts", "batch", "grp"), None),
            P(("parts", "batch", "grp"), None),
        ),
        check_vma=False,
    )
```

```python
import functools

import jax
import jax.numpy as jnp
from jax import lax
from jax.experimental import pallas as pl
from jax.experimental.pallas import tpu as pltpu
from jax.sharding import PartitionSpec as P

sharpness_factor = 20.0
norm_eps = 1e-06


def shortened(value):

    def short(part):
        return part.astype(jnp.bfloat16) if part.dtype == jnp.float32 else part

    return jax.tree.map(short, value)


def unit_rows(embedded):
    widened = embedded.astype(jnp.float32)
    inverse_norm = lax.rsqrt(jnp.sum(widened * widened, axis=1, keepdims=True) + norm_eps)
    return (widened * inverse_norm, inverse_norm)


def slot_layout(owner_table, owner_count, capacity):
    owner_list = owner_table.reshape(-1)
    onehot = (owner_list[:, None] == jnp.arange(owner_count, dtype=jnp.int32)[None, :]).astype(
        jnp.int32
    )
    before = jnp.cumsum(onehot, axis=0) - onehot
    rank_in_slot = jnp.sum(before * onehot, axis=1)
    slot_place = owner_list * capacity + rank_in_slot
    pair_query = jnp.arange(owner_list.shape[0], dtype=jnp.int32) // owner_table.shape[1]
    holder = (
        jnp.full((owner_count * capacity,), owner_table.shape[0], jnp.int32)
        .at[slot_place]
        .set(pair_query)
    )
    return (slot_place, holder)


def back_project(unit, inverse_norm, direction):
    inner = jnp.sum(unit * direction, axis=1, keepdims=True)
    return (inverse_norm * (direction - unit * inner)).astype(jnp.bfloat16)


def local_slots(queries, passages, hard_owners):
    query_unit, query_norm = unit_rows(queries)
    passage_unit, passage_norm = unit_rows(passages)
    query_half = query_unit.astype(jnp.bfloat16)
    passage_half = passage_unit.astype(jnp.bfloat16)
    query_rows, embed_width = queries.shape
    passage_rows = passages.shape[0]
    picks_each = hard_owners.shape[1]
    batch_count = lax.axis_size("batch")
    group_count = lax.axis_size("grp")
    capacity = max(2, min(query_rows, 4 * query_rows * picks_each // (3 * batch_count)))
    slot_place, holder = slot_layout(hard_owners, batch_count, capacity)
    padded_queries = jnp.concatenate(
        [query_half, jnp.zeros((1, embed_width), jnp.bfloat16)], axis=0
    )
    outgoing = padded_queries[holder].reshape(batch_count, capacity, embed_width)
    arrived = lax.all_to_all(outgoing, "batch", split_axis=0, concat_axis=0, tiled=True).reshape(
        batch_count * capacity, embed_width
    )
    seat_similarity_values = sharpness_factor * jnp.einsum(
        "md,cd->mc", arrived, passage_half, preferred_element_type=jnp.float32
    )
    passage_wide = passage_half.astype(jnp.float32)
    document_vectors_by_team = lax.all_gather(passage_half, "grp", axis=0, tiled=True)
    entering_similarities = sharpness_factor * jnp.einsum(
        "id,jd->ij", query_half, document_vectors_by_team, preferred_element_type=jnp.float32
    )
    column = (
        lax.axis_index("grp") * passage_rows
        + jnp.arange(query_rows, dtype=jnp.int32) % passage_rows
    )
    matching_indicator = (
        jnp.arange(group_count * passage_rows, dtype=jnp.int32)[None, :] == column[:, None]
    )
    totals_in = jnp.sum(jnp.exp(entering_similarities), axis=1)
    returned = lax.all_to_all(
        seat_similarity_values.reshape(batch_count, capacity, passage_rows).astype(jnp.bfloat16),
        "batch",
        split_axis=0,
        concat_axis=0,
        tiled=True,
    ).astype(jnp.float32)
    pair_scores = returned.reshape(batch_count * capacity, passage_rows)[slot_place]
    totals = totals_in + jnp.sum(
        jnp.exp(pair_scores).reshape(query_rows, picks_each * passage_rows), axis=1
    )
    normalizer_logarithm = jnp.log(totals)
    pair_weights = jnp.exp(pair_scores - jnp.repeat(normalizer_logarithm, picks_each)[:, None])
    weight_slots = (
        jnp.zeros((batch_count * capacity, passage_rows), jnp.float32)
        .at[slot_place]
        .set(pair_weights)
    )
    slot_weights = (
        lax.all_to_all(
            weight_slots.reshape(batch_count, capacity, passage_rows).astype(jnp.bfloat16),
            "batch",
            split_axis=0,
            concat_axis=0,
            tiled=True,
        )
        .astype(jnp.float32)
        .reshape(batch_count * capacity, passage_rows)
    )
    seat_backward_derivative = sharpness_factor * jnp.dot(
        slot_weights, passage_wide, precision=lax.Precision.HIGHEST
    )
    home_rows = lax.all_to_all(
        shortened(seat_backward_derivative.reshape(batch_count, capacity, embed_width)),
        "batch",
        split_axis=0,
        concat_axis=0,
        tiled=True,
    )
    pair_rows = home_rows.reshape(batch_count * capacity, embed_width)[slot_place]
    hard_dir = jnp.sum(pair_rows.reshape(query_rows, picks_each, embed_width), axis=1)
    hard_negative_documents = sharpness_factor * jnp.einsum(
        "mc,md->cd", slot_weights.astype(jnp.bfloat16), arrived, preferred_element_type=jnp.float32
    )
    query_loss = normalizer_logarithm - jnp.sum(
        jnp.where(matching_indicator, entering_similarities, 0.0), axis=1
    )
    upstream_derivative = (
        sharpness_factor
        * (
            jnp.exp(entering_similarities - normalizer_logarithm[:, None])
            - matching_indicator.astype(jnp.float32)
        )
    ).astype(jnp.bfloat16)
    query_dir = (
        jnp.dot(upstream_derivative, document_vectors_by_team, preferred_element_type=jnp.float32)
        + hard_dir
    )
    passage_dir = (
        lax.psum_scatter(
            jnp.einsum(
                "ij,id->jd", upstream_derivative, query_half, preferred_element_type=jnp.float32
            ).astype(jnp.bfloat16),
            "grp",
            scatter_dimension=0,
            tiled=True,
        ).astype(jnp.float32)
        + hard_negative_documents
    )
    return (
        query_loss,
        back_project(query_unit, query_norm, query_dir),
        back_project(passage_unit, passage_norm, passage_dir),
    )


def local_dense(queries, passages, hard_owners):
    query_unit, query_norm = unit_rows(queries)
    passage_unit, passage_norm = unit_rows(passages)
    query_half = query_unit.astype(jnp.bfloat16)
    passage_half = passage_unit.astype(jnp.bfloat16)
    query_rows = queries.shape[0]
    passage_rows = passages.shape[0]
    batch_count = lax.axis_size("batch")
    group_count = lax.axis_size("grp")
    group_blocks = lax.all_gather(passage_half, "grp", axis=0, tiled=True)
    line_blocks = lax.all_gather(passage_half, "batch", axis=0, tiled=True)
    scores_in = sharpness_factor * jnp.einsum(
        "id,jd->ij", query_half, group_blocks, preferred_element_type=jnp.float32
    )
    scores_hard = sharpness_factor * jnp.einsum(
        "id,jd->ij", query_half, line_blocks, preferred_element_type=jnp.float32
    )
    block = jnp.arange(batch_count * passage_rows, dtype=jnp.int32)[None, :] // passage_rows
    named = jnp.any(hard_owners[:, :, None] == block[:, None, :], axis=1)
    column = (
        lax.axis_index("grp") * passage_rows
        + jnp.arange(query_rows, dtype=jnp.int32) % passage_rows
    )
    positive = (
        jnp.arange(group_count * passage_rows, dtype=jnp.int32)[None, :] == column[:, None]
    )
    raised_in = jnp.exp(scores_in)
    raised_hard = jnp.where(named, jnp.exp(scores_hard), 0.0)
    totals = jnp.sum(raised_in, axis=1) + jnp.sum(raised_hard, axis=1)
    log_total = jnp.log(totals)
    query_loss = log_total - jnp.sum(jnp.where(positive, scores_in, 0.0), axis=1)
    scale = sharpness_factor / totals
    grad_in = (
        raised_in * scale[:, None] - jnp.where(positive, sharpness_factor, 0.0)
    ).astype(jnp.bfloat16)
    grad_hard = (raised_hard * scale[:, None]).astype(jnp.bfloat16)
    query_dir = jnp.dot(
        grad_in, group_blocks, preferred_element_type=jnp.float32
    ) + jnp.dot(grad_hard, line_blocks, preferred_element_type=jnp.float32)

    def summed(grad, axis):
        partial = jnp.einsum("ij,id->jd", grad, query_half, preferred_element_type=jnp.float32)
        return lax.psum_scatter(
            partial.astype(jnp.bfloat16), axis, scatter_dimension=0, tiled=True
        ).astype(jnp.float32)

    passage_dir = summed(grad_in, "grp") + summed(grad_hard, "batch")
    return (
        query_loss,
        back_project(query_unit, query_norm, query_dir),
        back_project(passage_unit, passage_norm, passage_dir),
    )


CHUNKS = 2
ROWS = 32
MESH = pl.DeviceIdType.MESH


def dot(left, right, left_dim, right_dim):
    return lax.dot_general(
        left,
        right,
        (((left_dim,), (right_dim,)), ((), ())),
        preferred_element_type=jnp.float32,
    )


def fused_kernel(
    nb, ng,
    queries_far, passages_far, owners,
    loss_out, query_out, passage_out,
    queries, passages, line, group, query_half, query_norm, passage_norm,
    grad_in, grad_hard, query_dir,
    hard_sums, from_left, from_right, in_sums, from_group,
    hard_parts, guest, guest_hard,
    load_sems, guest_send, guest_recv, weight_send, weight_recv,
    gather_send, gather_recv, group_send, group_recv,
    reduce_send, reduce_recv, back_send, back_recv,
):
    b = lax.axis_index("batch")
    g = lax.axis_index("grp")
    rows, width = queries.shape
    block = passages.shape[0]
    part = block // CHUNKS
    last = nb - 1

    def when(condition, act):
        pl.when(condition)(act)

    def piece(c):
        return pl.ds(c * part, part)

    def along(src, dst, send, recv, step):
        return pltpu.make_async_remote_copy(
            src_ref=src, dst_ref=dst, send_sem=send, recv_sem=recv,
            device_id={"batch": b + step}, device_id_type=MESH,
        )

    def gather(way, owner, s, c):
        ref = line.at[owner, piece(c)]
        return along(ref, ref, gather_send.at[way, s, c], gather_recv.at[way, s, c], 1 - 2 * way)

    def group_copy(src, dst, send, recv, k):
        return pltpu.make_async_remote_copy(
            src_ref=src, dst_ref=dst, send_sem=send.at[k], recv_sem=recv.at[k],
            device_id={"grp": lax.rem(g + k, ng)}, device_id_type=MESH,
        )

    def reduce(way, s, c):
        target = s if way else last - s
        landing = from_right if way else from_left
        return along(
            hard_sums.at[target, piece(c)], landing.at[s, piece(c)],
            reduce_send.at[way, s, c], reduce_recv.at[way, s, c], 1 - 2 * way,
        )

    inward = jnp.where(b == 0, 1, -1)

    def guest_copy(c):
        half = pl.ds(c * (rows // 2), rows // 2)
        return along(
            query_half.at[half], guest.at[half], guest_send.at[c], guest_recv.at[c], inward
        )

    def weight_copy(s):
        target = jnp.where(b == 0, last - s, s)
        return along(
            hard_parts.at[target], guest_hard.at[s], weight_send.at[s], weight_recv.at[s], inward
        )

    load_passages = pltpu.make_async_copy(passages_far, passages, load_sems.at[0])
    load_queries = pltpu.make_async_copy(queries_far, queries, load_sems.at[1])
    load_passages.start()
    load_queries.start()
    end = (b == 0) | (b == last)
    host = (b == 1) | (b == last - 1)
    barrier = pltpu.get_barrier_semaphore()

    def greet(step):
        pl.semaphore_signal(
            barrier, inc=1, device_id={"batch": b + step}, device_id_type=MESH
        )

    when(b > 0, lambda: greet(-1))
    when(b < last, lambda: greet(1))
    for k in range(1, ng):
        pl.semaphore_signal(
            barrier, inc=1, device_id={"grp": lax.rem(g + k, ng)}, device_id_type=MESH
        )

    def norm_passages(i, _):
        at = pl.ds(pl.multiple_of(i * ROWS, ROWS), ROWS)
        wide = passages[at, :].astype(jnp.float32)
        norm = lax.rsqrt(jnp.sum(wide * wide, axis=1, keepdims=True) + norm_eps)
        half = (wide * norm).astype(jnp.bfloat16)
        passage_norm[at, :] = norm
        line[b, at, :] = half
        group[g, at, :] = half
        return _

    load_passages.wait()
    lax.fori_loop(0, block // ROWS, norm_passages, 0)
    pl.semaphore_wait(
        barrier, ng - 1 + (b > 0).astype(jnp.int32) + (b < last).astype(jnp.int32)
    )
    for c in range(CHUNKS):
        when(b < last, lambda: gather(0, b, 0, c).start())
        when(b > 0, lambda: gather(1, b, 0, c).start())
    for k in range(1, ng):
        group_copy(group.at[g], group.at[g], group_send, group_recv, k).start()

    def norm_queries(i, _):
        at = pl.ds(pl.multiple_of(i * ROWS, ROWS), ROWS)
        wide = queries[at, :].astype(jnp.float32)
        norm = lax.rsqrt(jnp.sum(wide * wide, axis=1, keepdims=True) + norm_eps)
        query_norm[at, :] = norm
        query_half[at, :] = (wide * norm).astype(jnp.bfloat16)
        return _

    load_queries.wait()
    lax.fori_loop(0, rows // ROWS, norm_queries, 0)
    for c in range(2):
        when(end, lambda: guest_copy(c).start())

    def take(way, s, c):
        owner = b + 1 + s if way else b - 1 - s

        def pass_on():
            gather(way, owner, s + 1, c).start()

        def arrive():
            gather(way, owner, s, c).wait_recv()
            if s + 1 < last:
                when(b > 0 if way else b < last, pass_on)

        when(owner <= last if way else owner >= 0, arrive)

    for s in range(last):
        for c in range(CHUNKS):
            take(0, s, c)
            take(1, s, c)
    for k in range(1, ng):
        source = lax.rem(g + ng - k, ng)
        group_copy(
            group.at[source], group.at[source], group_send, group_recv, k
        ).wait_recv()

    units = query_half[...]
    scores_in = sharpness_factor * dot(
        units, group[...].reshape(ng * block, width), 1, 1
    )
    scores_hard = sharpness_factor * dot(
        units, line[...].reshape(nb * block, width), 1, 1
    )
    raised_in = jnp.exp(scores_in)
    square = (block, block)
    diagonal = lax.broadcasted_iota(jnp.int32, square, 0) == lax.broadcasted_iota(
        jnp.int32, square, 1
    )

    def upright(row):
        pieces = [
            jnp.sum(
                jnp.where(diagonal, row[:, i * block:(i + 1) * block], 0.0),
                axis=1,
                keepdims=True,
            )
            for i in range(rows // block)
        ]
        return jnp.concatenate(pieces, axis=0)

    names = [
        upright(owners[k:k + 1, :].astype(jnp.float32)) for k in range(owners.shape[0])
    ]
    raised_hard = []
    for n in range(nb):
        named = functools.reduce(jnp.logical_or, [name == n for name in names])
        raised_hard.append(
            jnp.where(named, jnp.exp(scores_hard[:, n * block:(n + 1) * block]), 0.0)
        )
    totals = jnp.sum(raised_in, axis=1, keepdims=True) + jnp.sum(
        functools.reduce(jnp.add, raised_hard), axis=1, keepdims=True
    )
    scale = sharpness_factor / totals
    for n in range(nb):
        weights = (raised_hard[n] * scale).astype(jnp.bfloat16)
        grad_hard[:, n * block:(n + 1) * block] = weights
        hard_parts[n] = weights
    for s in range(last):
        when(end, lambda: weight_copy(s).start())
    shape = (rows, ng * block)
    column = g * block + lax.rem(lax.broadcasted_iota(jnp.int32, shape, 0), block)
    positive = lax.broadcasted_iota(jnp.int32, shape, 1) == column
    losses = jnp.log(totals) - jnp.sum(
        jnp.where(positive, scores_in, 0.0), axis=1, keepdims=True
    )
    for i in range(rows // block):
        loss_out[i:i + 1, :] = jnp.sum(
            jnp.where(diagonal, losses[i * block:(i + 1) * block], 0.0), axis=0, keepdims=True
        )
    grad_in[...] = (
        raised_in * scale - jnp.where(positive, sharpness_factor, 0.0)
    ).astype(jnp.bfloat16)

    for n in sorted(range(nb), key=lambda n: -abs(2 * n - last)):
        hard_sums[n] = dot(
            grad_hard[:, n * block:(n + 1) * block], query_half[...], 0, 0
        ).astype(jnp.bfloat16)
    for h in range(ng):
        in_sums[h] = dot(
            grad_in[:, h * block:(h + 1) * block], query_half[...], 0, 0
        ).astype(jnp.bfloat16)

    def back_copy(k):
        return group_copy(
            in_sums.at[lax.rem(g + k, ng)], from_group.at[k - 1], back_send, back_recv, k
        )

    for k in range(1, ng):
        back_copy(k).start()

    tile = min(512, width)
    for j in range(0, width, tile):
        query_dir[:, j:j + tile] = dot(
            grad_in[...], group[:, :, j:j + tile].reshape(ng * block, tile), 1, 0
        ) + dot(grad_hard[...], line[:, :, j:j + tile].reshape(nb * block, tile), 1, 0)

    def finish_queries(i, _):
        at = pl.ds(pl.multiple_of(i * ROWS, ROWS), ROWS)
        norm = query_norm[at, :]
        unit = queries[at, :].astype(jnp.float32) * norm
        direction = query_dir[at, :]
        inner = jnp.sum(unit * direction, axis=1, keepdims=True)
        query_out[at, :] = (norm * (direction - unit * inner)).astype(jnp.bfloat16)
        return _

    lax.fori_loop(0, rows // ROWS, finish_queries, 0)

    def add_and_pass(way, s, c):
        target = s if way else last - s
        landing = from_right if way else from_left

        def act():
            reduce(way, s, c).wait_recv()
            own = hard_sums[target, piece(c), :].astype(jnp.float32)
            hard_sums[target, piece(c), :] = (
                own + landing[s, piece(c), :].astype(jnp.float32)
            ).astype(jnp.bfloat16)
            reduce(way, s, c).start()

        when((b < last - 1) & (b > target) if way else (b > 1) & (b < target), act)

    def add_guest(s):
        target = jnp.where(b == 1, last - s, s)
        weight_copy(s).wait_recv()
        for j in range(0, width, tile):
            cols = pl.ds(j, tile)
            own = hard_sums[target, :, cols].astype(jnp.float32)
            hard_sums[target, :, cols] = (
                own + dot(guest_hard[s], guest[:, cols], 0, 0)
            ).astype(jnp.bfloat16)
        if s < last - 1:
            for c in range(CHUNKS):
                when(b == 1, lambda: reduce(0, s, c).start())
                when(b == last - 1, lambda: reduce(1, s, c).start())

    def serve():
        for c in range(2):
            guest_copy(c).wait_recv()
        for s in range(last):
            add_guest(s)

    when(host, serve)
    for s in range(last - 1):
        for c in range(CHUNKS):
            add_and_pass(0, s, c)
            add_and_pass(1, s, c)
    for k in range(1, ng):
        back_copy(k).wait_recv()

    def finish_passages(at):
        total = hard_sums[b, at, :].astype(jnp.float32) + in_sums[g, at, :].astype(jnp.float32)
        for k in range(ng - 1):
            total += from_group[k, at, :].astype(jnp.float32)
        return total

    left_at = jnp.minimum(last - b, last - 2)
    right_at = jnp.minimum(b, last - 2)
    for c in range(CHUNKS):
        for way in (0, 1):
            for s in range(last - 1):
                target = s if way else last - s
                when(b == target, lambda: reduce(way, s, c).wait_recv())

        def finish(i, _):
            at = pl.ds(pl.multiple_of(c * part + i * ROWS, ROWS), ROWS)
            direction = finish_passages(at)
            direction += jnp.where(b > 1, from_left[left_at, at, :].astype(jnp.float32), 0.0)
            direction += jnp.where(b < last - 1, from_right[right_at, at, :].astype(jnp.float32), 0.0)
            norm = passage_norm[at, :]
            unit = passages[at, :].astype(jnp.float32) * norm
            inner = jnp.sum(unit * direction, axis=1, keepdims=True)
            passage_out[at, :] = (norm * (direction - unit * inner)).astype(jnp.bfloat16)
            return _

        lax.fori_loop(0, part // ROWS, finish, 0)

    for s in range(last):
        for c in range(CHUNKS):
            when((b < last) & (b >= s), lambda: gather(0, b - s, s, c).wait_send())
            when((b > 0) & (b + s <= last), lambda: gather(1, b + s, s, c).wait_send())
            if s < last - 1:
                when((b > 0) & (b < last - s), lambda: reduce(0, s, c).wait_send())
                when((b < last) & (b > s), lambda: reduce(1, s, c).wait_send())
        when(end, lambda: weight_copy(s).wait_send())
    for c in range(2):
        when(end, lambda: guest_copy(c).wait_send())
    for k in range(1, ng):
        group_copy(group.at[g], group.at[g], group_send, group_recv, k).wait_send()
        back_copy(k).wait_send()


def local_fused(queries, passages, hard_owners):
    rows, width = queries.shape
    block = passages.shape[0]
    nb, ng = lax.axis_size("batch"), lax.axis_size("grp")
    half, wide = jnp.bfloat16, jnp.float32
    vmem = pl.BlockSpec(memory_space=pltpu.VMEM)
    far = pl.BlockSpec(memory_space=pl.ANY)
    line_sems = pltpu.SemaphoreType.DMA((2, nb - 1, CHUNKS))
    sum_sems = pltpu.SemaphoreType.DMA((2, nb - 2, CHUNKS))
    pair_sems = pltpu.SemaphoreType.DMA((2,))
    weight_sems = pltpu.SemaphoreType.DMA((nb - 1,))
    group_sems = pltpu.SemaphoreType.DMA((ng,))
    loss, query_grad, passage_grad = pl.pallas_call(
        functools.partial(fused_kernel, nb, ng),
        out_shape=(
            jax.ShapeDtypeStruct((rows // block, block), wide),
            jax.ShapeDtypeStruct((rows, width), half),
            jax.ShapeDtypeStruct((block, width), half),
        ),
        in_specs=[far, far, vmem],
        out_specs=(vmem,) * 3,
        scratch_shapes=[
            pltpu.VMEM((rows, width), half),
            pltpu.VMEM((block, width), half),
            pltpu.VMEM((nb, block, width), half),
            pltpu.VMEM((ng, block, width), half),
            pltpu.VMEM((rows, width), half),
            pltpu.VMEM((rows, 1), wide),
            pltpu.VMEM((block, 1), wide),
            pltpu.VMEM((rows, ng * block), half),
            pltpu.VMEM((rows, nb * block), half),
            pltpu.VMEM((rows, width), wide),
            pltpu.VMEM((nb, block, width), half),
            pltpu.VMEM((nb - 2, block, width), half),
            pltpu.VMEM((nb - 2, block, width), half),
            pltpu.VMEM((ng, block, width), half),
            pltpu.VMEM((ng - 1, block, width), half),
            pltpu.VMEM((nb, rows, block), half),
            pltpu.VMEM((rows, width), half),
            pltpu.VMEM((nb - 1, rows, block), half),
            pair_sems, pair_sems, pair_sems, weight_sems, weight_sems,
            line_sems, line_sems, group_sems, group_sems,
            sum_sems, sum_sems, group_sems, group_sems,
        ],
        compiler_params=pltpu.CompilerParams(
            collective_id=0, has_side_effects=True, vmem_limit_bytes=56 * 1024 * 1024
        ),
        cost_estimate=pl.CostEstimate(
            flops=6 * rows * (nb + ng) * block * width,
            bytes_accessed=4 * (rows + block) * width,
            transcendentals=rows * (nb + ng) * block,
        ),
    )(queries, passages, hard_owners.T)
    return (loss.reshape(-1), query_grad, passage_grad)


def local(queries, passages, hard_owners):
    nb = lax.axis_size("batch")
    if 4 <= nb <= 8 and 1 < lax.axis_size("grp") <= 8:
        return local_fused(queries, passages, hard_owners)
    if nb <= 8:
        return local_dense(queries, passages, hard_owners)
    return local_slots(queries, passages, hard_owners)


def solution(mesh):
    placed = (
        P(("parts", "batch", "grp"), None),
        P(("parts", "batch", "grp"), None),
        P(("parts", "batch", "grp"), None),
    )
    return jax.shard_map(
        local,
        mesh=mesh,
        in_specs=placed,
        out_specs=(
            P(("parts", "batch", "grp")),
            P(("parts", "batch", "grp"), None),
            P(("parts", "batch", "grp"), None),
        ),
        check_vma=False,
    )
```

```python
import functools

import jax
import jax.numpy as jnp
from jax import lax
from jax.experimental import pallas as pl
from jax.experimental.pallas import tpu as pltpu
from jax.sharding import PartitionSpec as P

sharpness_factor = 20.0
norm_eps = 1e-06


def shortened(value):

    def short(part):
        return part.astype(jnp.bfloat16) if part.dtype == jnp.float32 else part

    return jax.tree.map(short, value)


def unit_rows(embedded):
    widened = embedded.astype(jnp.float32)
    inverse_norm = lax.rsqrt(jnp.sum(widened * widened, axis=1, keepdims=True) + norm_eps)
    return (widened * inverse_norm, inverse_norm)


def slot_layout(owner_table, owner_count, capacity):
    owner_list = owner_table.reshape(-1)
    onehot = (owner_list[:, None] == jnp.arange(owner_count, dtype=jnp.int32)[None, :]).astype(
        jnp.int32
    )
    before = jnp.cumsum(onehot, axis=0) - onehot
    rank_in_slot = jnp.sum(before * onehot, axis=1)
    slot_place = owner_list * capacity + rank_in_slot
    pair_query = jnp.arange(owner_list.shape[0], dtype=jnp.int32) // owner_table.shape[1]
    holder = (
        jnp.full((owner_count * capacity,), owner_table.shape[0], jnp.int32)
        .at[slot_place]
        .set(pair_query)
    )
    return (slot_place, holder)


def back_project(unit, inverse_norm, direction):
    inner = jnp.sum(unit * direction, axis=1, keepdims=True)
    return (inverse_norm * (direction - unit * inner)).astype(jnp.bfloat16)


def local_slots(queries, passages, hard_owners):
    query_unit, query_norm = unit_rows(queries)
    passage_unit, passage_norm = unit_rows(passages)
    query_half = query_unit.astype(jnp.bfloat16)
    passage_half = passage_unit.astype(jnp.bfloat16)
    query_rows, embed_width = queries.shape
    passage_rows = passages.shape[0]
    picks_each = hard_owners.shape[1]
    batch_count = lax.axis_size("batch")
    group_count = lax.axis_size("grp")
    capacity = max(2, min(query_rows, 4 * query_rows * picks_each // (3 * batch_count)))
    slot_place, holder = slot_layout(hard_owners, batch_count, capacity)
    padded_queries = jnp.concatenate(
        [query_half, jnp.zeros((1, embed_width), jnp.bfloat16)], axis=0
    )
    outgoing = padded_queries[holder].reshape(batch_count, capacity, embed_width)
    arrived = lax.all_to_all(outgoing, "batch", split_axis=0, concat_axis=0, tiled=True).reshape(
        batch_count * capacity, embed_width
    )
    seat_similarity_values = sharpness_factor * jnp.einsum(
        "md,cd->mc", arrived, passage_half, preferred_element_type=jnp.float32
    )
    passage_wide = passage_half.astype(jnp.float32)
    document_vectors_by_team = lax.all_gather(passage_half, "grp", axis=0, tiled=True)
    entering_similarities = sharpness_factor * jnp.einsum(
        "id,jd->ij", query_half, document_vectors_by_team, preferred_element_type=jnp.float32
    )
    column = (
        lax.axis_index("grp") * passage_rows
        + jnp.arange(query_rows, dtype=jnp.int32) % passage_rows
    )
    matching_indicator = (
        jnp.arange(group_count * passage_rows, dtype=jnp.int32)[None, :] == column[:, None]
    )
    totals_in = jnp.sum(jnp.exp(entering_similarities), axis=1)
    returned = lax.all_to_all(
        seat_similarity_values.reshape(batch_count, capacity, passage_rows).astype(jnp.bfloat16),
        "batch",
        split_axis=0,
        concat_axis=0,
        tiled=True,
    ).astype(jnp.float32)
    pair_scores = returned.reshape(batch_count * capacity, passage_rows)[slot_place]
    totals = totals_in + jnp.sum(
        jnp.exp(pair_scores).reshape(query_rows, picks_each * passage_rows), axis=1
    )
    normalizer_logarithm = jnp.log(totals)
    pair_weights = jnp.exp(pair_scores - jnp.repeat(normalizer_logarithm, picks_each)[:, None])
    weight_slots = (
        jnp.zeros((batch_count * capacity, passage_rows), jnp.float32)
        .at[slot_place]
        .set(pair_weights)
    )
    slot_weights = (
        lax.all_to_all(
            weight_slots.reshape(batch_count, capacity, passage_rows).astype(jnp.bfloat16),
            "batch",
            split_axis=0,
            concat_axis=0,
            tiled=True,
        )
        .astype(jnp.float32)
        .reshape(batch_count * capacity, passage_rows)
    )
    seat_backward_derivative = sharpness_factor * jnp.dot(
        slot_weights, passage_wide, precision=lax.Precision.HIGHEST
    )
    home_rows = lax.all_to_all(
        shortened(seat_backward_derivative.reshape(batch_count, capacity, embed_width)),
        "batch",
        split_axis=0,
        concat_axis=0,
        tiled=True,
    )
    pair_rows = home_rows.reshape(batch_count * capacity, embed_width)[slot_place]
    hard_dir = jnp.sum(pair_rows.reshape(query_rows, picks_each, embed_width), axis=1)
    hard_negative_documents = sharpness_factor * jnp.einsum(
        "mc,md->cd", slot_weights.astype(jnp.bfloat16), arrived, preferred_element_type=jnp.float32
    )
    query_loss = normalizer_logarithm - jnp.sum(
        jnp.where(matching_indicator, entering_similarities, 0.0), axis=1
    )
    upstream_derivative = (
        sharpness_factor
        * (
            jnp.exp(entering_similarities - normalizer_logarithm[:, None])
            - matching_indicator.astype(jnp.float32)
        )
    ).astype(jnp.bfloat16)
    query_dir = (
        jnp.dot(upstream_derivative, document_vectors_by_team, preferred_element_type=jnp.float32)
        + hard_dir
    )
    passage_dir = (
        lax.psum_scatter(
            jnp.einsum(
                "ij,id->jd", upstream_derivative, query_half, preferred_element_type=jnp.float32
            ).astype(jnp.bfloat16),
            "grp",
            scatter_dimension=0,
            tiled=True,
        ).astype(jnp.float32)
        + hard_negative_documents
    )
    return (
        query_loss,
        back_project(query_unit, query_norm, query_dir),
        back_project(passage_unit, passage_norm, passage_dir),
    )


def local_dense(queries, passages, hard_owners):
    query_unit, query_norm = unit_rows(queries)
    passage_unit, passage_norm = unit_rows(passages)
    query_half = query_unit.astype(jnp.bfloat16)
    passage_half = passage_unit.astype(jnp.bfloat16)
    query_rows = queries.shape[0]
    passage_rows = passages.shape[0]
    batch_count = lax.axis_size("batch")
    group_count = lax.axis_size("grp")
    group_blocks = lax.all_gather(passage_half, "grp", axis=0, tiled=True)
    line_blocks = lax.all_gather(passage_half, "batch", axis=0, tiled=True)
    scores_in = sharpness_factor * jnp.einsum(
        "id,jd->ij", query_half, group_blocks, preferred_element_type=jnp.float32
    )
    scores_hard = sharpness_factor * jnp.einsum(
        "id,jd->ij", query_half, line_blocks, preferred_element_type=jnp.float32
    )
    block = jnp.arange(batch_count * passage_rows, dtype=jnp.int32)[None, :] // passage_rows
    named = jnp.any(hard_owners[:, :, None] == block[:, None, :], axis=1)
    column = (
        lax.axis_index("grp") * passage_rows
        + jnp.arange(query_rows, dtype=jnp.int32) % passage_rows
    )
    positive = (
        jnp.arange(group_count * passage_rows, dtype=jnp.int32)[None, :] == column[:, None]
    )
    raised_in = jnp.exp(scores_in)
    raised_hard = jnp.where(named, jnp.exp(scores_hard), 0.0)
    totals = jnp.sum(raised_in, axis=1) + jnp.sum(raised_hard, axis=1)
    log_total = jnp.log(totals)
    query_loss = log_total - jnp.sum(jnp.where(positive, scores_in, 0.0), axis=1)
    scale = sharpness_factor / totals
    grad_in = (
        raised_in * scale[:, None] - jnp.where(positive, sharpness_factor, 0.0)
    ).astype(jnp.bfloat16)
    grad_hard = (raised_hard * scale[:, None]).astype(jnp.bfloat16)
    query_dir = jnp.dot(
        grad_in, group_blocks, preferred_element_type=jnp.float32
    ) + jnp.dot(grad_hard, line_blocks, preferred_element_type=jnp.float32)

    def summed(grad, axis):
        partial = jnp.einsum("ij,id->jd", grad, query_half, preferred_element_type=jnp.float32)
        return lax.psum_scatter(
            partial.astype(jnp.bfloat16), axis, scatter_dimension=0, tiled=True
        ).astype(jnp.float32)

    passage_dir = summed(grad_in, "grp") + summed(grad_hard, "batch")
    return (
        query_loss,
        back_project(query_unit, query_norm, query_dir),
        back_project(passage_unit, passage_norm, passage_dir),
    )


GATHER_CHUNKS = 2
SUM_CHUNKS = 2
ROWS = 32
MESH = pl.DeviceIdType.MESH


def dot(left, right, left_dim, right_dim):
    return lax.dot_general(
        left,
        right,
        (((left_dim,), (right_dim,)), ((), ())),
        preferred_element_type=jnp.float32,
    )


def fused_kernel(
    nb, ng,
    queries_far, passages_far, owners,
    loss_out, query_out, passage_out,
    queries, passages, line, group, query_half, query_norm, passage_norm,
    grad_in, grad_hard, query_dir,
    hard_sums, from_left, from_right, in_sums, from_group,
    hard_parts, guest, guest_hard,
    names, raised_hard, hard_total, raised_in, in_total, positive_score,
    load_sems, guest_send, guest_recv, weight_send, weight_recv,
    gather_send, gather_recv, group_send, group_recv,
    reduce_send, reduce_recv, back_send, back_recv,
):
    b = lax.axis_index("batch")
    g = lax.axis_index("grp")
    rows, width = queries.shape
    block = passages.shape[0]
    tile = min(512, width)
    last = nb - 1

    def when(condition, act):
        pl.when(condition)(act)

    def piece(c, count):
        return pl.ds(c * (block // count), block // count)

    def along(src, dst, send, recv, step):
        return pltpu.make_async_remote_copy(
            src_ref=src, dst_ref=dst, send_sem=send, recv_sem=recv,
            device_id={"batch": b + step}, device_id_type=MESH,
        )

    def gather(way, owner, s, c):
        ref = line.at[owner, piece(c, GATHER_CHUNKS)]
        return along(ref, ref, gather_send.at[way, s, c], gather_recv.at[way, s, c], 1 - 2 * way)

    def group_copy(src, dst, send, recv, k):
        return pltpu.make_async_remote_copy(
            src_ref=src, dst_ref=dst, send_sem=send.at[k], recv_sem=recv.at[k],
            device_id={"grp": lax.rem(g + k, ng)}, device_id_type=MESH,
        )

    def reduce(way, s, c):
        target = s if way else last - s
        landing = from_right if way else from_left
        return along(
            hard_sums.at[target, piece(c, SUM_CHUNKS)], landing.at[s, piece(c, SUM_CHUNKS)],
            reduce_send.at[way, s, c], reduce_recv.at[way, s, c], 1 - 2 * way,
        )

    inward = jnp.where(b == 0, 1, -1)

    def guest_copy(c):
        half = pl.ds(c * (rows // 2), rows // 2)
        return along(
            query_half.at[half], guest.at[half], guest_send.at[c], guest_recv.at[c], inward
        )

    def weight_copy(s):
        target = jnp.where(b == 0, last - s, s)
        return along(
            hard_parts.at[target], guest_hard.at[s], weight_send.at[s], weight_recv.at[s], inward
        )

    load_passages = pltpu.make_async_copy(passages_far, passages, load_sems.at[0])
    load_queries = pltpu.make_async_copy(queries_far, queries, load_sems.at[1])
    load_passages.start()
    load_queries.start()
    end = (b == 0) | (b == last)
    host = (b == 1) | (b == last - 1)
    barrier = pltpu.get_barrier_semaphore()

    def greet(step):
        pl.semaphore_signal(
            barrier, inc=1, device_id={"batch": b + step}, device_id_type=MESH
        )

    when(b > 0, lambda: greet(-1))
    when(b < last, lambda: greet(1))
    for k in range(1, ng):
        pl.semaphore_signal(
            barrier, inc=1, device_id={"grp": lax.rem(g + k, ng)}, device_id_type=MESH
        )

    def norm_passages(i, _):
        at = pl.ds(pl.multiple_of(i * ROWS, ROWS), ROWS)
        wide = passages[at, :].astype(jnp.float32)
        norm = lax.rsqrt(jnp.sum(wide * wide, axis=1, keepdims=True) + norm_eps)
        half = (wide * norm).astype(jnp.bfloat16)
        passage_norm[at, :] = norm
        line[b, at, :] = half
        group[g, at, :] = half
        return _

    load_passages.wait()
    lax.fori_loop(0, block // ROWS, norm_passages, 0)
    pl.semaphore_wait(
        barrier, ng - 1 + (b > 0).astype(jnp.int32) + (b < last).astype(jnp.int32)
    )
    for c in range(GATHER_CHUNKS):
        when(b < last, lambda: gather(0, b, 0, c).start())
        when(b > 0, lambda: gather(1, b, 0, c).start())
    for k in range(1, ng):
        group_copy(group.at[g], group.at[g], group_send, group_recv, k).start()

    def norm_queries(i, _):
        at = pl.ds(pl.multiple_of(i * ROWS, ROWS), ROWS)
        wide = queries[at, :].astype(jnp.float32)
        norm = lax.rsqrt(jnp.sum(wide * wide, axis=1, keepdims=True) + norm_eps)
        query_norm[at, :] = norm
        query_half[at, :] = (wide * norm).astype(jnp.bfloat16)
        return _

    load_queries.wait()
    lax.fori_loop(0, rows // ROWS, norm_queries, 0)
    for c in range(2):
        when(end, lambda: guest_copy(c).start())

    def take(way, s, c):
        owner = b + 1 + s if way else b - 1 - s

        def pass_on():
            gather(way, owner, s + 1, c).start()

        def arrive():
            gather(way, owner, s, c).wait_recv()
            if s + 1 < last:
                when(b > 0 if way else b < last, pass_on)

        when(owner <= last if way else owner >= 0, arrive)

    square = (block, block)
    diagonal = lax.broadcasted_iota(jnp.int32, square, 0) == lax.broadcasted_iota(
        jnp.int32, square, 1
    )

    def upright(row):
        pieces = [
            jnp.sum(
                jnp.where(diagonal, row[:, i * block:(i + 1) * block], 0.0),
                axis=1,
                keepdims=True,
            )
            for i in range(rows // block)
        ]
        return jnp.concatenate(pieces, axis=0)

    for k in range(owners.shape[0]):
        names[k] = upright(owners[k:k + 1, :].astype(jnp.float32))

    def score(n):
        raised = jnp.exp(sharpness_factor * dot(query_half[...], line[n], 1, 1))
        named = functools.reduce(
            jnp.logical_or,
            [names[k] == n.astype(jnp.float32) for k in range(owners.shape[0])],
        )
        raised = jnp.where(named, raised, 0.0)
        raised_hard[n] = raised
        hard_total[...] += raised

    hard_total[...] = jnp.zeros_like(hard_total)
    score(b)
    shape = (rows, ng * block)
    column = g * block + lax.rem(lax.broadcasted_iota(jnp.int32, shape, 0), block)
    for s in range(last):
        if s == last - 1:
            for k in range(1, ng):
                source = lax.rem(g + ng - k, ng)
                group_copy(
                    group.at[source], group.at[source], group_send, group_recv, k
                ).wait_recv()
            scores_in = sharpness_factor * dot(
                query_half[...], group[...].reshape(ng * block, width), 1, 1
            )
            raised = jnp.exp(scores_in)
            raised_in[...] = raised
            in_total[...] = jnp.sum(raised, axis=1, keepdims=True)
            positive = lax.broadcasted_iota(jnp.int32, shape, 1) == column
            positive_score[...] = jnp.sum(
                jnp.where(positive, scores_in, 0.0), axis=1, keepdims=True
            )
        for c in range(GATHER_CHUNKS):
            take(0, s, c)
            take(1, s, c)
        when(b - 1 - s >= 0, lambda: score(b - 1 - s))
        when(b + 1 + s <= last, lambda: score(b + 1 + s))

    totals = in_total[...] + jnp.sum(hard_total[...], axis=1, keepdims=True)
    scale = sharpness_factor / totals
    for n in range(nb):
        weights = (raised_hard[n] * scale).astype(jnp.bfloat16)
        grad_hard[:, n * block:(n + 1) * block] = weights
        hard_parts[n] = weights
    for s in range(last):
        when(end, lambda: weight_copy(s).start())
    losses = jnp.log(totals) - positive_score[...]
    for i in range(rows // block):
        loss_out[i * block:(i + 1) * block] = jnp.sum(
            jnp.where(diagonal, losses[i * block:(i + 1) * block], 0.0), axis=0
        )
    positive = lax.broadcasted_iota(jnp.int32, shape, 1) == column
    grad_in[...] = (
        raised_in[...] * scale - jnp.where(positive, sharpness_factor, 0.0)
    ).astype(jnp.bfloat16)

    for n in sorted(range(nb), key=lambda n: -abs(2 * n - last)):
        hard_sums[n] = dot(
            grad_hard[:, n * block:(n + 1) * block], query_half[...], 0, 0
        ).astype(jnp.bfloat16)
    for h in range(ng):
        in_sums[h] = dot(
            grad_in[:, h * block:(h + 1) * block], query_half[...], 0, 0
        ).astype(jnp.bfloat16)

    def back_copy(k):
        return group_copy(
            in_sums.at[lax.rem(g + k, ng)], from_group.at[k - 1], back_send, back_recv, k
        )

    for k in range(1, ng):
        back_copy(k).start()

    for j in range(0, width, tile):
        query_dir[:, j:j + tile] = dot(
            grad_in[...], group[:, :, j:j + tile].reshape(ng * block, tile), 1, 0
        ) + dot(grad_hard[...], line[:, :, j:j + tile].reshape(nb * block, tile), 1, 0)

    def finish_queries(i, _):
        at = pl.ds(pl.multiple_of(i * ROWS, ROWS), ROWS)
        norm = query_norm[at, :]
        unit = queries[at, :].astype(jnp.float32) * norm
        direction = query_dir[at, :]
        inner = jnp.sum(unit * direction, axis=1, keepdims=True)
        query_out[at, :] = (norm * (direction - unit * inner)).astype(jnp.bfloat16)
        return _

    lax.fori_loop(0, rows // ROWS, finish_queries, 0)

    def add_and_pass(way, s, c):
        target = s if way else last - s
        landing = from_right if way else from_left

        def act():
            reduce(way, s, c).wait_recv()
            own = hard_sums[target, piece(c, SUM_CHUNKS), :].astype(jnp.float32)
            hard_sums[target, piece(c, SUM_CHUNKS), :] = (
                own + landing[s, piece(c, SUM_CHUNKS), :].astype(jnp.float32)
            ).astype(jnp.bfloat16)
            reduce(way, s, c).start()

        when((b < last - 1) & (b > target) if way else (b > 1) & (b < target), act)

    def add_guest(s):
        target = jnp.where(b == 1, last - s, s)
        weight_copy(s).wait_recv()
        for j in range(0, width, tile):
            cols = pl.ds(j, tile)
            own = hard_sums[target, :, cols].astype(jnp.float32)
            hard_sums[target, :, cols] = (
                own + dot(guest_hard[s], guest[:, cols], 0, 0)
            ).astype(jnp.bfloat16)
        if s < last - 1:
            for c in range(SUM_CHUNKS):
                when(b == 1, lambda: reduce(0, s, c).start())
                when(b == last - 1, lambda: reduce(1, s, c).start())

    def serve():
        for c in range(2):
            guest_copy(c).wait_recv()
        for s in range(last):
            add_guest(s)

    when(host, serve)
    for s in range(last - 1):
        for c in range(SUM_CHUNKS):
            add_and_pass(0, s, c)
            add_and_pass(1, s, c)
    for k in range(1, ng):
        back_copy(k).wait_recv()

    def finish_passages(at):
        total = hard_sums[b, at, :].astype(jnp.float32) + in_sums[g, at, :].astype(jnp.float32)
        for k in range(ng - 1):
            total += from_group[k, at, :].astype(jnp.float32)
        return total

    left_at = jnp.minimum(last - b, last - 2)
    right_at = jnp.minimum(b, last - 2)
    for c in range(SUM_CHUNKS):
        for way in (0, 1):
            for s in range(last - 1):
                target = s if way else last - s
                when(b == target, lambda: reduce(way, s, c).wait_recv())

        def finish(i, _):
            at = pl.ds(pl.multiple_of(c * (block // SUM_CHUNKS) + i * ROWS, ROWS), ROWS)
            direction = finish_passages(at)
            direction += jnp.where(b > 1, from_left[left_at, at, :].astype(jnp.float32), 0.0)
            direction += jnp.where(b < last - 1, from_right[right_at, at, :].astype(jnp.float32), 0.0)
            norm = passage_norm[at, :]
            unit = passages[at, :].astype(jnp.float32) * norm
            inner = jnp.sum(unit * direction, axis=1, keepdims=True)
            passage_out[at, :] = (norm * (direction - unit * inner)).astype(jnp.bfloat16)
            return _

        lax.fori_loop(0, block // SUM_CHUNKS // ROWS, finish, 0)

    for s in range(last):
        for c in range(GATHER_CHUNKS):
            when((b < last) & (b >= s), lambda: gather(0, b - s, s, c).wait_send())
            when((b > 0) & (b + s <= last), lambda: gather(1, b + s, s, c).wait_send())
        when(end, lambda: weight_copy(s).wait_send())
    for s in range(last - 1):
        for c in range(SUM_CHUNKS):
            when((b > 0) & (b < last - s), lambda: reduce(0, s, c).wait_send())
            when((b < last) & (b > s), lambda: reduce(1, s, c).wait_send())
    for c in range(2):
        when(end, lambda: guest_copy(c).wait_send())
    for k in range(1, ng):
        group_copy(group.at[g], group.at[g], group_send, group_recv, k).wait_send()
        back_copy(k).wait_send()


def local_fused(queries, passages, hard_owners):
    rows, width = queries.shape
    block = passages.shape[0]
    nb, ng = lax.axis_size("batch"), lax.axis_size("grp")
    half, wide = jnp.bfloat16, jnp.float32
    vmem = pl.BlockSpec(memory_space=pltpu.VMEM)
    far = pl.BlockSpec(memory_space=pl.ANY)
    line_sems = pltpu.SemaphoreType.DMA((2, nb - 1, GATHER_CHUNKS))
    sum_sems = pltpu.SemaphoreType.DMA((2, nb - 2, SUM_CHUNKS))
    pair_sems = pltpu.SemaphoreType.DMA((2,))
    weight_sems = pltpu.SemaphoreType.DMA((nb - 1,))
    group_sems = pltpu.SemaphoreType.DMA((ng,))
    loss, query_grad, passage_grad = pl.pallas_call(
        functools.partial(fused_kernel, nb, ng),
        out_shape=(
            jax.ShapeDtypeStruct((rows,), wide),
            jax.ShapeDtypeStruct((rows, width), half),
            jax.ShapeDtypeStruct((block, width), half),
        ),
        in_specs=[far, far, vmem],
        out_specs=(vmem,) * 3,
        scratch_shapes=[
            pltpu.VMEM((rows, width), half),
            pltpu.VMEM((block, width), half),
            pltpu.VMEM((nb, block, width), half),
            pltpu.VMEM((ng, block, width), half),
            pltpu.VMEM((rows, width), half),
            pltpu.VMEM((rows, 1), wide),
            pltpu.VMEM((block, 1), wide),
            pltpu.VMEM((rows, ng * block), half),
            pltpu.VMEM((rows, nb * block), half),
            pltpu.VMEM((rows, width), wide),
            pltpu.VMEM((nb, block, width), half),
            pltpu.VMEM((nb - 2, block, width), half),
            pltpu.VMEM((nb - 2, block, width), half),
            pltpu.VMEM((ng, block, width), half),
            pltpu.VMEM((ng - 1, block, width), half),
            pltpu.VMEM((nb, rows, block), half),
            pltpu.VMEM((rows, width), half),
            pltpu.VMEM((nb - 1, rows, block), half),
            pltpu.VMEM((hard_owners.shape[1], rows, 1), wide),
            pltpu.VMEM((nb, rows, block), wide),
            pltpu.VMEM((rows, block), wide),
            pltpu.VMEM((rows, ng * block), wide),
            pltpu.VMEM((rows, 1), wide),
            pltpu.VMEM((rows, 1), wide),
            pair_sems, pair_sems, pair_sems, weight_sems, weight_sems,
            line_sems, line_sems, group_sems, group_sems,
            sum_sems, sum_sems, group_sems, group_sems,
        ],
        compiler_params=pltpu.CompilerParams(
            collective_id=0, has_side_effects=True, vmem_limit_bytes=56 * 1024 * 1024
        ),
        cost_estimate=pl.CostEstimate(
            flops=6 * rows * (nb + ng) * block * width,
            bytes_accessed=4 * (rows + block) * width,
            transcendentals=rows * (nb + ng) * block,
        ),
    )(queries, passages, hard_owners.T)
    return (loss, query_grad, passage_grad)


def local(queries, passages, hard_owners):
    nb = lax.axis_size("batch")
    if 4 <= nb <= 8 and 1 < lax.axis_size("grp") <= 8:
        return local_fused(queries, passages, hard_owners)
    if nb <= 8:
        return local_dense(queries, passages, hard_owners)
    return local_slots(queries, passages, hard_owners)


def solution(mesh):
    placed = (
        P(("parts", "batch", "grp"), None),
        P(("parts", "batch", "grp"), None),
        P(("parts", "batch", "grp"), None),
    )
    return jax.shard_map(
        local,
        mesh=mesh,
        in_specs=placed,
        out_specs=(
            P(("parts", "batch", "grp")),
            P(("parts", "batch", "grp"), None),
            P(("parts", "batch", "grp"), None),
        ),
        check_vma=False,
    )
```

```python
import functools

import jax
import jax.numpy as jnp
from jax import lax
from jax.experimental import pallas as pl
from jax.experimental.pallas import tpu as pltpu
from jax.sharding import PartitionSpec as P

sharpness_factor = 20.0
norm_eps = 1e-06


def shortened(value):

    def short(part):
        return part.astype(jnp.bfloat16) if part.dtype == jnp.float32 else part

    return jax.tree.map(short, value)


def unit_rows(embedded):
    widened = embedded.astype(jnp.float32)
    inverse_norm = lax.rsqrt(jnp.sum(widened * widened, axis=1, keepdims=True) + norm_eps)
    return (widened * inverse_norm, inverse_norm)


def slot_layout(owner_table, owner_count, capacity):
    owner_list = owner_table.reshape(-1)
    onehot = (owner_list[:, None] == jnp.arange(owner_count, dtype=jnp.int32)[None, :]).astype(
        jnp.int32
    )
    before = jnp.cumsum(onehot, axis=0) - onehot
    rank_in_slot = jnp.sum(before * onehot, axis=1)
    slot_place = owner_list * capacity + rank_in_slot
    pair_query = jnp.arange(owner_list.shape[0], dtype=jnp.int32) // owner_table.shape[1]
    holder = (
        jnp.full((owner_count * capacity,), owner_table.shape[0], jnp.int32)
        .at[slot_place]
        .set(pair_query)
    )
    return (slot_place, holder)


def back_project(unit, inverse_norm, direction):
    inner = jnp.sum(unit * direction, axis=1, keepdims=True)
    return (inverse_norm * (direction - unit * inner)).astype(jnp.bfloat16)


def local_slots(queries, passages, hard_owners):
    query_unit, query_norm = unit_rows(queries)
    passage_unit, passage_norm = unit_rows(passages)
    query_half = query_unit.astype(jnp.bfloat16)
    passage_half = passage_unit.astype(jnp.bfloat16)
    query_rows, embed_width = queries.shape
    passage_rows = passages.shape[0]
    picks_each = hard_owners.shape[1]
    batch_count = lax.axis_size("batch")
    group_count = lax.axis_size("grp")
    capacity = max(2, min(query_rows, 4 * query_rows * picks_each // (3 * batch_count)))
    slot_place, holder = slot_layout(hard_owners, batch_count, capacity)
    padded_queries = jnp.concatenate(
        [query_half, jnp.zeros((1, embed_width), jnp.bfloat16)], axis=0
    )
    outgoing = padded_queries[holder].reshape(batch_count, capacity, embed_width)
    arrived = lax.all_to_all(outgoing, "batch", split_axis=0, concat_axis=0, tiled=True).reshape(
        batch_count * capacity, embed_width
    )
    seat_similarity_values = sharpness_factor * jnp.einsum(
        "md,cd->mc", arrived, passage_half, preferred_element_type=jnp.float32
    )
    passage_wide = passage_half.astype(jnp.float32)
    document_vectors_by_team = lax.all_gather(passage_half, "grp", axis=0, tiled=True)
    entering_similarities = sharpness_factor * jnp.einsum(
        "id,jd->ij", query_half, document_vectors_by_team, preferred_element_type=jnp.float32
    )
    column = (
        lax.axis_index("grp") * passage_rows
        + jnp.arange(query_rows, dtype=jnp.int32) % passage_rows
    )
    matching_indicator = (
        jnp.arange(group_count * passage_rows, dtype=jnp.int32)[None, :] == column[:, None]
    )
    totals_in = jnp.sum(jnp.exp(entering_similarities), axis=1)
    returned = lax.all_to_all(
        seat_similarity_values.reshape(batch_count, capacity, passage_rows).astype(jnp.bfloat16),
        "batch",
        split_axis=0,
        concat_axis=0,
        tiled=True,
    ).astype(jnp.float32)
    pair_scores = returned.reshape(batch_count * capacity, passage_rows)[slot_place]
    totals = totals_in + jnp.sum(
        jnp.exp(pair_scores).reshape(query_rows, picks_each * passage_rows), axis=1
    )
    normalizer_logarithm = jnp.log(totals)
    pair_weights = jnp.exp(pair_scores - jnp.repeat(normalizer_logarithm, picks_each)[:, None])
    weight_slots = (
        jnp.zeros((batch_count * capacity, passage_rows), jnp.float32)
        .at[slot_place]
        .set(pair_weights)
    )
    slot_weights = (
        lax.all_to_all(
            weight_slots.reshape(batch_count, capacity, passage_rows).astype(jnp.bfloat16),
            "batch",
            split_axis=0,
            concat_axis=0,
            tiled=True,
        )
        .astype(jnp.float32)
        .reshape(batch_count * capacity, passage_rows)
    )
    seat_backward_derivative = sharpness_factor * jnp.dot(
        slot_weights, passage_wide, precision=lax.Precision.HIGHEST
    )
    home_rows = lax.all_to_all(
        shortened(seat_backward_derivative.reshape(batch_count, capacity, embed_width)),
        "batch",
        split_axis=0,
        concat_axis=0,
        tiled=True,
    )
    pair_rows = home_rows.reshape(batch_count * capacity, embed_width)[slot_place]
    hard_dir = jnp.sum(pair_rows.reshape(query_rows, picks_each, embed_width), axis=1)
    hard_negative_documents = sharpness_factor * jnp.einsum(
        "mc,md->cd", slot_weights.astype(jnp.bfloat16), arrived, preferred_element_type=jnp.float32
    )
    query_loss = normalizer_logarithm - jnp.sum(
        jnp.where(matching_indicator, entering_similarities, 0.0), axis=1
    )
    upstream_derivative = (
        sharpness_factor
        * (
            jnp.exp(entering_similarities - normalizer_logarithm[:, None])
            - matching_indicator.astype(jnp.float32)
        )
    ).astype(jnp.bfloat16)
    query_dir = (
        jnp.dot(upstream_derivative, document_vectors_by_team, preferred_element_type=jnp.float32)
        + hard_dir
    )
    passage_dir = (
        lax.psum_scatter(
            jnp.einsum(
                "ij,id->jd", upstream_derivative, query_half, preferred_element_type=jnp.float32
            ).astype(jnp.bfloat16),
            "grp",
            scatter_dimension=0,
            tiled=True,
        ).astype(jnp.float32)
        + hard_negative_documents
    )
    return (
        query_loss,
        back_project(query_unit, query_norm, query_dir),
        back_project(passage_unit, passage_norm, passage_dir),
    )


def local_dense(queries, passages, hard_owners):
    query_unit, query_norm = unit_rows(queries)
    passage_unit, passage_norm = unit_rows(passages)
    query_half = query_unit.astype(jnp.bfloat16)
    passage_half = passage_unit.astype(jnp.bfloat16)
    query_rows = queries.shape[0]
    passage_rows = passages.shape[0]
    batch_count = lax.axis_size("batch")
    group_count = lax.axis_size("grp")
    group_blocks = lax.all_gather(passage_half, "grp", axis=0, tiled=True)
    line_blocks = lax.all_gather(passage_half, "batch", axis=0, tiled=True)
    scores_in = sharpness_factor * jnp.einsum(
        "id,jd->ij", query_half, group_blocks, preferred_element_type=jnp.float32
    )
    scores_hard = sharpness_factor * jnp.einsum(
        "id,jd->ij", query_half, line_blocks, preferred_element_type=jnp.float32
    )
    block = jnp.arange(batch_count * passage_rows, dtype=jnp.int32)[None, :] // passage_rows
    named = jnp.any(hard_owners[:, :, None] == block[:, None, :], axis=1)
    column = (
        lax.axis_index("grp") * passage_rows
        + jnp.arange(query_rows, dtype=jnp.int32) % passage_rows
    )
    positive = (
        jnp.arange(group_count * passage_rows, dtype=jnp.int32)[None, :] == column[:, None]
    )
    raised_in = jnp.exp(scores_in)
    raised_hard = jnp.where(named, jnp.exp(scores_hard), 0.0)
    totals = jnp.sum(raised_in, axis=1) + jnp.sum(raised_hard, axis=1)
    log_total = jnp.log(totals)
    query_loss = log_total - jnp.sum(jnp.where(positive, scores_in, 0.0), axis=1)
    scale = sharpness_factor / totals
    grad_in = (
        raised_in * scale[:, None] - jnp.where(positive, sharpness_factor, 0.0)
    ).astype(jnp.bfloat16)
    grad_hard = (raised_hard * scale[:, None]).astype(jnp.bfloat16)
    query_dir = jnp.dot(
        grad_in, group_blocks, preferred_element_type=jnp.float32
    ) + jnp.dot(grad_hard, line_blocks, preferred_element_type=jnp.float32)

    def summed(grad, axis):
        partial = jnp.einsum("ij,id->jd", grad, query_half, preferred_element_type=jnp.float32)
        return lax.psum_scatter(
            partial.astype(jnp.bfloat16), axis, scatter_dimension=0, tiled=True
        ).astype(jnp.float32)

    passage_dir = summed(grad_in, "grp") + summed(grad_hard, "batch")
    return (
        query_loss,
        back_project(query_unit, query_norm, query_dir),
        back_project(passage_unit, passage_norm, passage_dir),
    )


PIECES = 3
ROWS = 32
MESH = pl.DeviceIdType.MESH


def dot(left, right, left_dim, right_dim):
    return lax.dot_general(
        left,
        right,
        (((left_dim,), (right_dim,)), ((), ())),
        preferred_element_type=jnp.float32,
    )


def fused_kernel(
    nb, ng,
    queries_far, passages_far, owners,
    loss_out, query_out, passage_out,
    queries, passages, line, group, query_half, query_norm, passage_norm,
    grad_in, grad_hard, query_dir,
    hard_sums, from_left, from_right, in_sums, from_group,
    hard_parts, guest, guest_hard, share_out, share_in,
    names, raised_hard, hard_total, raised_in, in_total, positive_score,
    load_sems, guest_send, guest_recv, weight_send, weight_recv, share_send, share_recv,
    gather_send, gather_recv, group_send, group_recv,
    reduce_send, reduce_recv, back_send, back_recv,
):
    b = lax.axis_index("batch")
    g = lax.axis_index("grp")
    rows, width = queries.shape
    block = passages.shape[0]
    tile = min(512, width)
    last = nb - 1

    def when(condition, act):
        pl.when(condition)(act)

    low, near = width // 8 * 3, width // 8 * 5
    columns = (pl.ds(0, low), pl.ds(low, near - low), pl.ds(near, width - near))
    halves = (pl.ds(0, near), pl.ds(near, width - near))

    def along(src, dst, send, recv, step):
        return pltpu.make_async_remote_copy(
            src_ref=src, dst_ref=dst, send_sem=send, recv_sem=recv,
            device_id={"batch": b + step}, device_id_type=MESH,
        )

    def gather(way, owner, s, c):
        ref = line.at[owner, :, halves[c]]
        return along(ref, ref, gather_send.at[way, s, c], gather_recv.at[way, s, c], 1 - 2 * way)

    def group_copy(src, dst, send, recv, k):
        return pltpu.make_async_remote_copy(
            src_ref=src, dst_ref=dst, send_sem=send.at[k], recv_sem=recv.at[k],
            device_id={"grp": lax.rem(g + k, ng)}, device_id_type=MESH,
        )

    def reduce(way, s, c):
        target = s if way else last - s
        landing = from_right if way else from_left
        return along(
            hard_sums.at[target, :, columns[c]], landing.at[s, :, columns[c]],
            reduce_send.at[way, s, c], reduce_recv.at[way, s, c], 1 - 2 * way,
        )

    inward = jnp.where(b == 0, 1, -1)

    def guest_copy(c):
        return along(
            query_half.at[:, columns[c]], guest.at[:, columns[c]],
            guest_send.at[c], guest_recv.at[c], inward,
        )

    outward = jnp.where((b == 1) | (b == last), -1, 1)

    def share_copy(s):
        return along(
            share_out.at[s], share_in.at[s], share_send.at[s], share_recv.at[s], outward
        )

    def weight_copy(s):
        target = jnp.where(b == 0, last - s, s)
        return along(
            hard_parts.at[target], guest_hard.at[s], weight_send.at[s], weight_recv.at[s], inward
        )

    load_passages = pltpu.make_async_copy(passages_far, passages, load_sems.at[0])
    load_queries = pltpu.make_async_copy(queries_far, queries, load_sems.at[1])
    load_passages.start()
    load_queries.start()
    end = (b == 0) | (b == last)
    host = (b == 1) | (b == last - 1)
    barrier = pltpu.get_barrier_semaphore()

    def greet(step):
        pl.semaphore_signal(
            barrier, inc=1, device_id={"batch": b + step}, device_id_type=MESH
        )

    when(b > 0, lambda: greet(-1))
    when(b < last, lambda: greet(1))
    for k in range(1, ng):
        pl.semaphore_signal(
            barrier, inc=1, device_id={"grp": lax.rem(g + k, ng)}, device_id_type=MESH
        )

    def norm_passages(i, _):
        at = pl.ds(pl.multiple_of(i * ROWS, ROWS), ROWS)
        wide = passages[at, :].astype(jnp.float32)
        norm = lax.rsqrt(jnp.sum(wide * wide, axis=1, keepdims=True) + norm_eps)
        half = (wide * norm).astype(jnp.bfloat16)
        passage_norm[at, :] = norm
        line[b, at, :] = half
        group[g, at, :] = half
        return _

    load_passages.wait()
    lax.fori_loop(0, block // ROWS, norm_passages, 0)
    pl.semaphore_wait(
        barrier, ng - 1 + (b > 0).astype(jnp.int32) + (b < last).astype(jnp.int32)
    )
    when(b < last, lambda: gather(0, b, 0, 0).start())
    when(b > 0, lambda: gather(1, b, 0, 0).start())
    when(b < last - 1, lambda: gather(0, b, 0, 1).start())
    when(b > 1, lambda: gather(1, b, 0, 1).start())
    for k in range(1, ng):
        group_copy(group.at[g], group.at[g], group_send, group_recv, k).start()

    def norm_queries(i, _):
        at = pl.ds(pl.multiple_of(i * ROWS, ROWS), ROWS)
        wide = queries[at, :].astype(jnp.float32)
        norm = lax.rsqrt(jnp.sum(wide * wide, axis=1, keepdims=True) + norm_eps)
        query_norm[at, :] = norm
        query_half[at, :] = (wide * norm).astype(jnp.bfloat16)
        return _

    load_queries.wait()
    lax.fori_loop(0, rows // ROWS, norm_queries, 0)
    when(end, lambda: guest_copy(2).start())

    def take(way, s, c):
        owner = b + 1 + s if way else b - 1 - s

        def pass_on():
            gather(way, owner, s + 1, c).start()

        def arrive():
            gather(way, owner, s, c).wait_recv()
            if s + 1 < last:
                when(b > c if way else b < last - c, pass_on)

        here = owner <= last if way else owner >= 0
        if c:
            here &= b > 0 if way else b < last
        when(here, arrive)

    square = (block, block)
    diagonal = lax.broadcasted_iota(jnp.int32, square, 0) == lax.broadcasted_iota(
        jnp.int32, square, 1
    )

    def upright(row):
        pieces = [
            jnp.sum(
                jnp.where(diagonal, row[:, i * block:(i + 1) * block], 0.0),
                axis=1,
                keepdims=True,
            )
            for i in range(rows // block)
        ]
        return jnp.concatenate(pieces, axis=0)

    for k in range(owners.shape[0]):
        names[k] = upright(owners[k:k + 1, :].astype(jnp.float32))

    def named(n):
        return functools.reduce(
            jnp.logical_or,
            [names[k] == n.astype(jnp.float32) for k in range(owners.shape[0])],
        )

    def score(n):
        raised = jnp.exp(sharpness_factor * dot(query_half[...], line[n], 1, 1))
        raised = jnp.where(named(n), raised, 0.0)
        raised_hard[n] = raised
        hard_total[...] += raised

    def score_near(n):
        raised_hard[n] = sharpness_factor * dot(
            query_half[:, halves[0]], line[n, :, halves[0]], 1, 1
        )

    def score_rest(s):
        n = jnp.where(b == 0, 1 + s, last - 1 - s)
        share_copy(s).wait_recv()
        raised = jnp.exp(raised_hard[n] + share_in[s].astype(jnp.float32))
        raised = jnp.where(named(n), raised, 0.0)
        raised_hard[n] = raised
        hard_total[...] += raised

    def share(s):
        n = jnp.where(b == 1, 1 + s, last - 1 - s)
        share_out[s] = (
            sharpness_factor * dot(guest[:, halves[1]], line[n, :, halves[1]], 1, 1)
        ).astype(jnp.bfloat16)
        share_copy(s).start()

    def share_early():
        guest_copy(2).wait_recv()
        for s in range(last - 1):
            share(s)

    def share_late():
        share(last - 1)
        for s in range(last):
            when(b == last - 1, lambda: gather(0, last - 1 - s, s, 1).start())
            when(b == 1, lambda: gather(1, 1 + s, s, 1).start())

    hard_total[...] = jnp.zeros_like(hard_total)
    score(b)
    shape = (rows, ng * block)
    column = g * block + lax.rem(lax.broadcasted_iota(jnp.int32, shape, 0), block)
    for s in range(last):
        if s == last - 1:
            for k in range(1, ng):
                source = lax.rem(g + ng - k, ng)
                group_copy(
                    group.at[source], group.at[source], group_send, group_recv, k
                ).wait_recv()
            scores_in = sharpness_factor * dot(
                query_half[...], group[...].reshape(ng * block, width), 1, 1
            )
            raised = jnp.exp(scores_in)
            raised_in[...] = raised
            in_total[...] = jnp.sum(raised, axis=1, keepdims=True)
            positive = lax.broadcasted_iota(jnp.int32, shape, 1) == column
            positive_score[...] = jnp.sum(
                jnp.where(positive, scores_in, 0.0), axis=1, keepdims=True
            )
        for c in range(2):
            take(0, s, c)
            take(1, s, c)
            if s == last - 2:
                when(host, share_late if c else share_early)
        left, right = b - 1 - s, b + 1 + s
        when((left >= 0) & (b < last), lambda: score(left))
        when((right <= last) & (b > 0), lambda: score(right))
        when((left >= 0) & (b == last), lambda: score_near(left))
        when((right <= last) & (b == 0), lambda: score_near(right))
        if s == min(1, last - 1):
            when(end, lambda: guest_copy(1).start())
    for s in range(last):
        when(end, lambda: score_rest(s))

    totals = in_total[...] + jnp.sum(hard_total[...], axis=1, keepdims=True)
    scale = sharpness_factor / totals
    for n in range(nb):
        weights = (raised_hard[n] * scale).astype(jnp.bfloat16)
        grad_hard[:, n * block:(n + 1) * block] = weights
        hard_parts[n] = weights
    for s in range(last):
        when(end, lambda: weight_copy(s).start())
    when(end, lambda: guest_copy(0).start())
    losses = jnp.log(totals) - positive_score[...]
    for i in range(rows // block):
        loss_out[i * block:(i + 1) * block] = jnp.sum(
            jnp.where(diagonal, losses[i * block:(i + 1) * block], 0.0), axis=0
        )
    positive = lax.broadcasted_iota(jnp.int32, shape, 1) == column
    grad_in[...] = (
        raised_in[...] * scale - jnp.where(positive, sharpness_factor, 0.0)
    ).astype(jnp.bfloat16)

    for n in sorted(range(nb), key=lambda n: -abs(2 * n - last)):
        hard_sums[n] = dot(
            grad_hard[:, n * block:(n + 1) * block], query_half[...], 0, 0
        ).astype(jnp.bfloat16)
    for h in range(ng):
        in_sums[h] = dot(
            grad_in[:, h * block:(h + 1) * block], query_half[...], 0, 0
        ).astype(jnp.bfloat16)

    def back_copy(k):
        return group_copy(
            in_sums.at[lax.rem(g + k, ng)], from_group.at[k - 1], back_send, back_recv, k
        )

    for k in range(1, ng):
        back_copy(k).start()

    def add_and_pass(way, s, c):
        target = s if way else last - s
        landing = from_right if way else from_left

        def act():
            reduce(way, s, c).wait_recv()
            own = hard_sums[target, :, columns[c]].astype(jnp.float32)
            hard_sums[target, :, columns[c]] = (
                own + landing[s, :, columns[c]].astype(jnp.float32)
            ).astype(jnp.bfloat16)
            reduce(way, s, c).start()

        when((b < last - 1) & (b > target) if way else (b > 1) & (b < target), act)

    def serve(c):
        guest_copy(c).wait_recv() if c < 2 else None
        for s in range(last):
            target = jnp.where(b == 1, last - s, s)
            if c == 2:
                weight_copy(s).wait_recv()
            own = hard_sums[target, :, columns[c]].astype(jnp.float32)
            hard_sums[target, :, columns[c]] = (
                own + dot(guest_hard[s], guest[:, columns[c]], 0, 0)
            ).astype(jnp.bfloat16)
            if s < last - 1:
                when(b == 1, lambda: reduce(0, s, c).start())
                when(b == last - 1, lambda: reduce(1, s, c).start())

    when(host, lambda: serve(2))
    when(host, lambda: serve(1))
    for s in range(last):
        when(b == last, lambda: gather(0, last - 1 - s, s, 1).wait_recv())
        when(b == 0, lambda: gather(1, 1 + s, s, 1).wait_recv())

    for j in range(0, width, tile):
        query_dir[:, j:j + tile] = dot(
            grad_in[...], group[:, :, j:j + tile].reshape(ng * block, tile), 1, 0
        ) + dot(grad_hard[...], line[:, :, j:j + tile].reshape(nb * block, tile), 1, 0)

    def finish_queries(i, _):
        at = pl.ds(pl.multiple_of(i * ROWS, ROWS), ROWS)
        norm = query_norm[at, :]
        unit = queries[at, :].astype(jnp.float32) * norm
        direction = query_dir[at, :]
        inner = jnp.sum(unit * direction, axis=1, keepdims=True)
        query_out[at, :] = (norm * (direction - unit * inner)).astype(jnp.bfloat16)
        return _

    lax.fori_loop(0, rows // ROWS, finish_queries, 0)

    for c in (2, 1, 0):
        if c == 1:
            when(host, lambda: serve(0))
        for s in range(last - 1):
            add_and_pass(0, s, c)
            add_and_pass(1, s, c)
    for k in range(1, ng):
        back_copy(k).wait_recv()

    def finish_passages(at):
        total = hard_sums[b, at, :].astype(jnp.float32) + in_sums[g, at, :].astype(jnp.float32)
        for k in range(ng - 1):
            total += from_group[k, at, :].astype(jnp.float32)
        return total

    left_at = jnp.minimum(last - b, last - 2)
    right_at = jnp.minimum(b, last - 2)
    for c in range(PIECES):
        for way in (0, 1):
            for s in range(last - 1):
                target = s if way else last - s
                when(b == target, lambda: reduce(way, s, c).wait_recv())

    def finish(i, _):
        at = pl.ds(pl.multiple_of(i * ROWS, ROWS), ROWS)
        direction = finish_passages(at)
        direction += jnp.where(b > 1, from_left[left_at, at, :].astype(jnp.float32), 0.0)
        direction += jnp.where(b < last - 1, from_right[right_at, at, :].astype(jnp.float32), 0.0)
        norm = passage_norm[at, :]
        unit = passages[at, :].astype(jnp.float32) * norm
        inner = jnp.sum(unit * direction, axis=1, keepdims=True)
        passage_out[at, :] = (norm * (direction - unit * inner)).astype(jnp.bfloat16)
        return _

    lax.fori_loop(0, block // ROWS, finish, 0)

    for s in range(last):
        for c in range(2):
            when((b < last) & (b >= s), lambda: gather(0, b - s, s, c).wait_send())
            when((b > 0) & (b + s <= last), lambda: gather(1, b + s, s, c).wait_send())
        when(end, lambda: weight_copy(s).wait_send())
        when(host, lambda: share_copy(s).wait_send())
    for s in range(last - 1):
        for c in range(PIECES):
            when((b > 0) & (b < last - s), lambda: reduce(0, s, c).wait_send())
            when((b < last) & (b > s), lambda: reduce(1, s, c).wait_send())
    for c in range(PIECES):
        when(end, lambda: guest_copy(c).wait_send())
    for k in range(1, ng):
        group_copy(group.at[g], group.at[g], group_send, group_recv, k).wait_send()
        back_copy(k).wait_send()


def local_fused(queries, passages, hard_owners):
    rows, width = queries.shape
    block = passages.shape[0]
    nb, ng = lax.axis_size("batch"), lax.axis_size("grp")
    half, wide = jnp.bfloat16, jnp.float32
    vmem = pl.BlockSpec(memory_space=pltpu.VMEM)
    far = pl.BlockSpec(memory_space=pl.ANY)
    line_sems = pltpu.SemaphoreType.DMA((2, nb - 1, 2))
    sum_sems = pltpu.SemaphoreType.DMA((2, nb - 2, PIECES))
    pair_sems = pltpu.SemaphoreType.DMA((2,))
    guest_sems = pltpu.SemaphoreType.DMA((PIECES,))
    weight_sems = pltpu.SemaphoreType.DMA((nb - 1,))
    group_sems = pltpu.SemaphoreType.DMA((ng,))
    loss, query_grad, passage_grad = pl.pallas_call(
        functools.partial(fused_kernel, nb, ng),
        out_shape=(
            jax.ShapeDtypeStruct((rows,), wide),
            jax.ShapeDtypeStruct((rows, width), half),
            jax.ShapeDtypeStruct((block, width), half),
        ),
        in_specs=[far, far, vmem],
        out_specs=(vmem,) * 3,
        scratch_shapes=[
            pltpu.VMEM((rows, width), half),
            pltpu.VMEM((block, width), half),
            pltpu.VMEM((nb, block, width), half),
            pltpu.VMEM((ng, block, width), half),
            pltpu.VMEM((rows, width), half),
            pltpu.VMEM((rows, 1), wide),
            pltpu.VMEM((block, 1), wide),
            pltpu.VMEM((rows, ng * block), half),
            pltpu.VMEM((rows, nb * block), half),
            pltpu.VMEM((rows, width), wide),
            pltpu.VMEM((nb, block, width), half),
            pltpu.VMEM((nb - 2, block, width), half),
            pltpu.VMEM((nb - 2, block, width), half),
            pltpu.VMEM((ng, block, width), half),
            pltpu.VMEM((ng - 1, block, width), half),
            pltpu.VMEM((nb, rows, block), half),
            pltpu.VMEM((rows, width), half),
            pltpu.VMEM((nb - 1, rows, block), half),
            pltpu.VMEM((nb - 1, rows, block), half),
            pltpu.VMEM((nb - 1, rows, block), half),
            pltpu.VMEM((hard_owners.shape[1], rows, 1), wide),
            pltpu.VMEM((nb, rows, block), wide),
            pltpu.VMEM((rows, block), wide),
            pltpu.VMEM((rows, ng * block), wide),
            pltpu.VMEM((rows, 1), wide),
            pltpu.VMEM((rows, 1), wide),
            pair_sems, guest_sems, guest_sems, weight_sems, weight_sems, weight_sems, weight_sems,
            line_sems, line_sems, group_sems, group_sems,
            sum_sems, sum_sems, group_sems, group_sems,
        ],
        compiler_params=pltpu.CompilerParams(
            collective_id=0, has_side_effects=True, vmem_limit_bytes=56 * 1024 * 1024
        ),
        cost_estimate=pl.CostEstimate(
            flops=6 * rows * (nb + ng) * block * width,
            bytes_accessed=4 * (rows + block) * width,
            transcendentals=rows * (nb + ng) * block,
        ),
    )(queries, passages, hard_owners.T)
    return (loss, query_grad, passage_grad)


def local(queries, passages, hard_owners):
    nb = lax.axis_size("batch")
    if queries.shape[1] % 1024 == 0 and 4 <= nb <= 8 and 1 < lax.axis_size("grp") <= 8:
        return local_fused(queries, passages, hard_owners)
    if nb <= 8:
        return local_dense(queries, passages, hard_owners)
    return local_slots(queries, passages, hard_owners)


def solution(mesh):
    placed = (
        P(("parts", "batch", "grp"), None),
        P(("parts", "batch", "grp"), None),
        P(("parts", "batch", "grp"), None),
    )
    return jax.shard_map(
        local,
        mesh=mesh,
        in_specs=placed,
        out_specs=(
            P(("parts", "batch", "grp")),
            P(("parts", "batch", "grp"), None),
            P(("parts", "batch", "grp"), None),
        ),
        check_vma=False,
    )
```

```python
import functools

import jax
import jax.numpy as jnp
from jax import lax
from jax.experimental import pallas as pl
from jax.experimental.pallas import tpu as pltpu
from jax.sharding import PartitionSpec as P

sharpness_factor = 20.0
norm_eps = 1e-06


def shortened(value):

    def short(part):
        return part.astype(jnp.bfloat16) if part.dtype == jnp.float32 else part

    return jax.tree.map(short, value)


def unit_rows(embedded):
    widened = embedded.astype(jnp.float32)
    inverse_norm = lax.rsqrt(jnp.sum(widened * widened, axis=1, keepdims=True) + norm_eps)
    return (widened * inverse_norm, inverse_norm)


def slot_layout(owner_table, owner_count, capacity):
    owner_list = owner_table.reshape(-1)
    onehot = (owner_list[:, None] == jnp.arange(owner_count, dtype=jnp.int32)[None, :]).astype(
        jnp.int32
    )
    before = jnp.cumsum(onehot, axis=0) - onehot
    rank_in_slot = jnp.sum(before * onehot, axis=1)
    slot_place = owner_list * capacity + rank_in_slot
    pair_query = jnp.arange(owner_list.shape[0], dtype=jnp.int32) // owner_table.shape[1]
    holder = (
        jnp.full((owner_count * capacity,), owner_table.shape[0], jnp.int32)
        .at[slot_place]
        .set(pair_query)
    )
    return (slot_place, holder)


def back_project(unit, inverse_norm, direction):
    inner = jnp.sum(unit * direction, axis=1, keepdims=True)
    return (inverse_norm * (direction - unit * inner)).astype(jnp.bfloat16)


def local_slots(queries, passages, hard_owners):
    query_unit, query_norm = unit_rows(queries)
    passage_unit, passage_norm = unit_rows(passages)
    query_half = query_unit.astype(jnp.bfloat16)
    passage_half = passage_unit.astype(jnp.bfloat16)
    query_rows, embed_width = queries.shape
    passage_rows = passages.shape[0]
    picks_each = hard_owners.shape[1]
    batch_count = lax.axis_size("batch")
    group_count = lax.axis_size("grp")
    capacity = max(2, min(query_rows, 4 * query_rows * picks_each // (3 * batch_count)))
    slot_place, holder = slot_layout(hard_owners, batch_count, capacity)
    padded_queries = jnp.concatenate(
        [query_half, jnp.zeros((1, embed_width), jnp.bfloat16)], axis=0
    )
    outgoing = padded_queries[holder].reshape(batch_count, capacity, embed_width)
    arrived = lax.all_to_all(outgoing, "batch", split_axis=0, concat_axis=0, tiled=True).reshape(
        batch_count * capacity, embed_width
    )
    seat_similarity_values = sharpness_factor * jnp.einsum(
        "md,cd->mc", arrived, passage_half, preferred_element_type=jnp.float32
    )
    passage_wide = passage_half.astype(jnp.float32)
    document_vectors_by_team = lax.all_gather(passage_half, "grp", axis=0, tiled=True)
    entering_similarities = sharpness_factor * jnp.einsum(
        "id,jd->ij", query_half, document_vectors_by_team, preferred_element_type=jnp.float32
    )
    column = (
        lax.axis_index("grp") * passage_rows
        + jnp.arange(query_rows, dtype=jnp.int32) % passage_rows
    )
    matching_indicator = (
        jnp.arange(group_count * passage_rows, dtype=jnp.int32)[None, :] == column[:, None]
    )
    totals_in = jnp.sum(jnp.exp(entering_similarities), axis=1)
    returned = lax.all_to_all(
        seat_similarity_values.reshape(batch_count, capacity, passage_rows).astype(jnp.bfloat16),
        "batch",
        split_axis=0,
        concat_axis=0,
        tiled=True,
    ).astype(jnp.float32)
    pair_scores = returned.reshape(batch_count * capacity, passage_rows)[slot_place]
    totals = totals_in + jnp.sum(
        jnp.exp(pair_scores).reshape(query_rows, picks_each * passage_rows), axis=1
    )
    normalizer_logarithm = jnp.log(totals)
    pair_weights = jnp.exp(pair_scores - jnp.repeat(normalizer_logarithm, picks_each)[:, None])
    weight_slots = (
        jnp.zeros((batch_count * capacity, passage_rows), jnp.float32)
        .at[slot_place]
        .set(pair_weights)
    )
    slot_weights = (
        lax.all_to_all(
            weight_slots.reshape(batch_count, capacity, passage_rows).astype(jnp.bfloat16),
            "batch",
            split_axis=0,
            concat_axis=0,
            tiled=True,
        )
        .astype(jnp.float32)
        .reshape(batch_count * capacity, passage_rows)
    )
    seat_backward_derivative = sharpness_factor * jnp.dot(
        slot_weights, passage_wide, precision=lax.Precision.HIGHEST
    )
    home_rows = lax.all_to_all(
        shortened(seat_backward_derivative.reshape(batch_count, capacity, embed_width)),
        "batch",
        split_axis=0,
        concat_axis=0,
        tiled=True,
    )
    pair_rows = home_rows.reshape(batch_count * capacity, embed_width)[slot_place]
    hard_dir = jnp.sum(pair_rows.reshape(query_rows, picks_each, embed_width), axis=1)
    hard_negative_documents = sharpness_factor * jnp.einsum(
        "mc,md->cd", slot_weights.astype(jnp.bfloat16), arrived, preferred_element_type=jnp.float32
    )
    query_loss = normalizer_logarithm - jnp.sum(
        jnp.where(matching_indicator, entering_similarities, 0.0), axis=1
    )
    upstream_derivative = (
        sharpness_factor
        * (
            jnp.exp(entering_similarities - normalizer_logarithm[:, None])
            - matching_indicator.astype(jnp.float32)
        )
    ).astype(jnp.bfloat16)
    query_dir = (
        jnp.dot(upstream_derivative, document_vectors_by_team, preferred_element_type=jnp.float32)
        + hard_dir
    )
    passage_dir = (
        lax.psum_scatter(
            jnp.einsum(
                "ij,id->jd", upstream_derivative, query_half, preferred_element_type=jnp.float32
            ).astype(jnp.bfloat16),
            "grp",
            scatter_dimension=0,
            tiled=True,
        ).astype(jnp.float32)
        + hard_negative_documents
    )
    return (
        query_loss,
        back_project(query_unit, query_norm, query_dir),
        back_project(passage_unit, passage_norm, passage_dir),
    )


def local_dense(queries, passages, hard_owners):
    query_unit, query_norm = unit_rows(queries)
    passage_unit, passage_norm = unit_rows(passages)
    query_half = query_unit.astype(jnp.bfloat16)
    passage_half = passage_unit.astype(jnp.bfloat16)
    query_rows = queries.shape[0]
    passage_rows = passages.shape[0]
    batch_count = lax.axis_size("batch")
    group_count = lax.axis_size("grp")
    group_blocks = lax.all_gather(passage_half, "grp", axis=0, tiled=True)
    line_blocks = lax.all_gather(passage_half, "batch", axis=0, tiled=True)
    scores_in = sharpness_factor * jnp.einsum(
        "id,jd->ij", query_half, group_blocks, preferred_element_type=jnp.float32
    )
    scores_hard = sharpness_factor * jnp.einsum(
        "id,jd->ij", query_half, line_blocks, preferred_element_type=jnp.float32
    )
    block = jnp.arange(batch_count * passage_rows, dtype=jnp.int32)[None, :] // passage_rows
    named = jnp.any(hard_owners[:, :, None] == block[:, None, :], axis=1)
    column = (
        lax.axis_index("grp") * passage_rows
        + jnp.arange(query_rows, dtype=jnp.int32) % passage_rows
    )
    positive = (
        jnp.arange(group_count * passage_rows, dtype=jnp.int32)[None, :] == column[:, None]
    )
    raised_in = jnp.exp(scores_in)
    raised_hard = jnp.where(named, jnp.exp(scores_hard), 0.0)
    totals = jnp.sum(raised_in, axis=1) + jnp.sum(raised_hard, axis=1)
    log_total = jnp.log(totals)
    query_loss = log_total - jnp.sum(jnp.where(positive, scores_in, 0.0), axis=1)
    scale = sharpness_factor / totals
    grad_in = (
        raised_in * scale[:, None] - jnp.where(positive, sharpness_factor, 0.0)
    ).astype(jnp.bfloat16)
    grad_hard = (raised_hard * scale[:, None]).astype(jnp.bfloat16)
    query_dir = jnp.dot(
        grad_in, group_blocks, preferred_element_type=jnp.float32
    ) + jnp.dot(grad_hard, line_blocks, preferred_element_type=jnp.float32)

    def summed(grad, axis):
        partial = jnp.einsum("ij,id->jd", grad, query_half, preferred_element_type=jnp.float32)
        return lax.psum_scatter(
            partial.astype(jnp.bfloat16), axis, scatter_dimension=0, tiled=True
        ).astype(jnp.float32)

    passage_dir = summed(grad_in, "grp") + summed(grad_hard, "batch")
    return (
        query_loss,
        back_project(query_unit, query_norm, query_dir),
        back_project(passage_unit, passage_norm, passage_dir),
    )


PIECES = 3
ROWS = 32
MESH = pl.DeviceIdType.MESH


def dot(left, right, left_dim, right_dim):
    return lax.dot_general(
        left,
        right,
        (((left_dim,), (right_dim,)), ((), ())),
        preferred_element_type=jnp.float32,
    )


def fused_kernel(
    nb, ng,
    queries_far, passages_far, owners,
    loss_out, query_out, passage_out,
    queries, passages, line, group, query_half, query_norm, passage_norm,
    grad_in, grad_hard, query_dir,
    hard_sums, from_left, from_right, in_sums, from_group,
    hard_parts, guest, guest_hard, share_out, share_in,
    names, raised_hard, hard_total, raised_in, in_total, positive_score,
    load_sems, guest_send, guest_recv, weight_send, weight_recv, share_send, share_recv,
    gather_send, gather_recv, group_send, group_recv,
    reduce_send, reduce_recv, back_send, back_recv,
):
    b = lax.axis_index("batch")
    g = lax.axis_index("grp")
    rows, width = queries.shape
    block = passages.shape[0]
    tile = min(512, width)
    last = nb - 1

    def when(condition, act):
        pl.when(condition)(act)

    low, near = width // 8 * 2, width // 8 * 4
    columns = (pl.ds(0, low), pl.ds(low, near - low), pl.ds(near, width - near))
    halves = (pl.ds(0, near), pl.ds(near, width - near))

    def along(src, dst, send, recv, step):
        return pltpu.make_async_remote_copy(
            src_ref=src, dst_ref=dst, send_sem=send, recv_sem=recv,
            device_id={"batch": b + step}, device_id_type=MESH,
        )

    def gather(way, owner, s, c):
        ref = line.at[owner, :, halves[c]]
        return along(ref, ref, gather_send.at[way, s, c], gather_recv.at[way, s, c], 1 - 2 * way)

    def group_copy(src, dst, send, recv, k):
        return pltpu.make_async_remote_copy(
            src_ref=src, dst_ref=dst, send_sem=send.at[k], recv_sem=recv.at[k],
            device_id={"grp": lax.rem(g + k, ng)}, device_id_type=MESH,
        )

    def reduce(way, s, c):
        target = s if way else last - s
        landing = from_right if way else from_left
        return along(
            hard_sums.at[target, :, columns[c]], landing.at[s, :, columns[c]],
            reduce_send.at[way, s, c], reduce_recv.at[way, s, c], 1 - 2 * way,
        )

    inward = jnp.where(b == 0, 1, -1)

    def guest_copy(c):
        return along(
            query_half.at[:, columns[c]], guest.at[:, columns[c]],
            guest_send.at[c], guest_recv.at[c], inward,
        )

    outward = jnp.where((b == 1) | (b == last), -1, 1)

    def share_copy(s):
        return along(
            share_out.at[s], share_in.at[s], share_send.at[s], share_recv.at[s], outward
        )

    def weight_copy(s):
        target = jnp.where(b == 0, last - s, s)
        return along(
            hard_parts.at[target], guest_hard.at[s], weight_send.at[s], weight_recv.at[s], inward
        )

    load_passages = pltpu.make_async_copy(passages_far, passages, load_sems.at[0])
    load_queries = pltpu.make_async_copy(queries_far, queries, load_sems.at[1])
    load_passages.start()
    load_queries.start()
    end = (b == 0) | (b == last)
    host = (b == 1) | (b == last - 1)
    barrier = pltpu.get_barrier_semaphore()

    def greet(step):
        pl.semaphore_signal(
            barrier, inc=1, device_id={"batch": b + step}, device_id_type=MESH
        )

    when(b > 0, lambda: greet(-1))
    when(b < last, lambda: greet(1))
    for k in range(1, ng):
        pl.semaphore_signal(
            barrier, inc=1, device_id={"grp": lax.rem(g + k, ng)}, device_id_type=MESH
        )

    def norm_passages(i, _):
        at = pl.ds(pl.multiple_of(i * ROWS, ROWS), ROWS)
        wide = passages[at, :].astype(jnp.float32)
        norm = lax.rsqrt(jnp.sum(wide * wide, axis=1, keepdims=True) + norm_eps)
        half = (wide * norm).astype(jnp.bfloat16)
        passage_norm[at, :] = norm
        line[b, at, :] = half
        group[g, at, :] = half
        return _

    load_passages.wait()
    lax.fori_loop(0, block // ROWS, norm_passages, 0)
    pl.semaphore_wait(
        barrier, ng - 1 + (b > 0).astype(jnp.int32) + (b < last).astype(jnp.int32)
    )
    when(b < last, lambda: gather(0, b, 0, 0).start())
    when(b > 0, lambda: gather(1, b, 0, 0).start())
    when(b < last - 1, lambda: gather(0, b, 0, 1).start())
    when(b > 1, lambda: gather(1, b, 0, 1).start())
    for k in range(1, ng):
        group_copy(group.at[g], group.at[g], group_send, group_recv, k).start()

    def norm_queries(i, _):
        at = pl.ds(pl.multiple_of(i * ROWS, ROWS), ROWS)
        wide = queries[at, :].astype(jnp.float32)
        norm = lax.rsqrt(jnp.sum(wide * wide, axis=1, keepdims=True) + norm_eps)
        query_norm[at, :] = norm
        query_half[at, :] = (wide * norm).astype(jnp.bfloat16)
        return _

    load_queries.wait()
    lax.fori_loop(0, rows // ROWS, norm_queries, 0)
    when(end, lambda: guest_copy(2).start())

    def take(way, s, c):
        owner = b + 1 + s if way else b - 1 - s

        def pass_on():
            gather(way, owner, s + 1, c).start()

        def arrive():
            gather(way, owner, s, c).wait_recv()
            if s + 1 < last:
                when(b > c if way else b < last - c, pass_on)

        here = owner <= last if way else owner >= 0
        if c:
            here &= b > 0 if way else b < last
        when(here, arrive)

    square = (block, block)
    diagonal = lax.broadcasted_iota(jnp.int32, square, 0) == lax.broadcasted_iota(
        jnp.int32, square, 1
    )

    def upright(row):
        pieces = [
            jnp.sum(
                jnp.where(diagonal, row[:, i * block:(i + 1) * block], 0.0),
                axis=1,
                keepdims=True,
            )
            for i in range(rows // block)
        ]
        return jnp.concatenate(pieces, axis=0)

    for k in range(owners.shape[0]):
        names[k] = upright(owners[k:k + 1, :].astype(jnp.float32))

    def named(n):
        return functools.reduce(
            jnp.logical_or,
            [names[k] == n.astype(jnp.float32) for k in range(owners.shape[0])],
        )

    def score(n):
        raised = jnp.exp(sharpness_factor * dot(query_half[...], line[n], 1, 1))
        raised = jnp.where(named(n), raised, 0.0)
        raised_hard[n] = raised
        hard_total[...] += raised

    def score_near(n):
        raised_hard[n] = sharpness_factor * dot(
            query_half[:, halves[0]], line[n, :, halves[0]], 1, 1
        )

    def score_rest(s):
        n = jnp.where(b == 0, 1 + s, last - 1 - s)
        share_copy(s).wait_recv()
        raised = jnp.exp(raised_hard[n] + share_in[s].astype(jnp.float32))
        raised = jnp.where(named(n), raised, 0.0)
        raised_hard[n] = raised
        hard_total[...] += raised

    def share(s):
        n = jnp.where(b == 1, 1 + s, last - 1 - s)
        share_out[s] = (
            sharpness_factor * dot(guest[:, halves[1]], line[n, :, halves[1]], 1, 1)
        ).astype(jnp.bfloat16)
        share_copy(s).start()

    def share_early():
        guest_copy(2).wait_recv()
        for s in range(last - 1):
            share(s)

    def share_late():
        share(last - 1)
        for s in range(last):
            when(b == last - 1, lambda: gather(0, last - 1 - s, s, 1).start())
            when(b == 1, lambda: gather(1, 1 + s, s, 1).start())

    hard_total[...] = jnp.zeros_like(hard_total)
    score(b)
    shape = (rows, ng * block)
    column = g * block + lax.rem(lax.broadcasted_iota(jnp.int32, shape, 0), block)
    for s in range(last):
        if s == last - 1:
            for k in range(1, ng):
                source = lax.rem(g + ng - k, ng)
                group_copy(
                    group.at[source], group.at[source], group_send, group_recv, k
                ).wait_recv()
            scores_in = sharpness_factor * dot(
                query_half[...], group[...].reshape(ng * block, width), 1, 1
            )
            raised = jnp.exp(scores_in)
            raised_in[...] = raised
            in_total[...] = jnp.sum(raised, axis=1, keepdims=True)
            positive = lax.broadcasted_iota(jnp.int32, shape, 1) == column
            positive_score[...] = jnp.sum(
                jnp.where(positive, scores_in, 0.0), axis=1, keepdims=True
            )
        for c in range(2):
            take(0, s, c)
            take(1, s, c)
            if s == last - 2:
                when(host, share_late if c else share_early)
        left, right = b - 1 - s, b + 1 + s
        when((left >= 0) & (b < last), lambda: score(left))
        when((right <= last) & (b > 0), lambda: score(right))
        when((left >= 0) & (b == last), lambda: score_near(left))
        when((right <= last) & (b == 0), lambda: score_near(right))
        if s == min(1, last - 1):
            when(end, lambda: guest_copy(1).start())
    for s in range(last):
        when(end, lambda: score_rest(s))

    totals = in_total[...] + jnp.sum(hard_total[...], axis=1, keepdims=True)
    scale = sharpness_factor / totals
    for n in range(nb):
        weights = (raised_hard[n] * scale).astype(jnp.bfloat16)
        grad_hard[:, n * block:(n + 1) * block] = weights
        hard_parts[n] = weights
    for s in range(last):
        when(end, lambda: weight_copy(s).start())
    when(end, lambda: guest_copy(0).start())
    losses = jnp.log(totals) - positive_score[...]
    for i in range(rows // block):
        loss_out[i * block:(i + 1) * block] = jnp.sum(
            jnp.where(diagonal, losses[i * block:(i + 1) * block], 0.0), axis=0
        )
    positive = lax.broadcasted_iota(jnp.int32, shape, 1) == column
    grad_in[...] = (
        raised_in[...] * scale - jnp.where(positive, sharpness_factor, 0.0)
    ).astype(jnp.bfloat16)

    for n in sorted(range(nb), key=lambda n: -abs(2 * n - last)):
        hard_sums[n] = dot(
            grad_hard[:, n * block:(n + 1) * block], query_half[...], 0, 0
        ).astype(jnp.bfloat16)
    for h in range(ng):
        in_sums[h] = dot(
            grad_in[:, h * block:(h + 1) * block], query_half[...], 0, 0
        ).astype(jnp.bfloat16)

    def back_copy(k):
        return group_copy(
            in_sums.at[lax.rem(g + k, ng)], from_group.at[k - 1], back_send, back_recv, k
        )

    for k in range(1, ng):
        back_copy(k).start()

    def add_and_pass(way, s, c):
        target = s if way else last - s
        landing = from_right if way else from_left

        def act():
            reduce(way, s, c).wait_recv()
            own = hard_sums[target, :, columns[c]].astype(jnp.float32)
            hard_sums[target, :, columns[c]] = (
                own + landing[s, :, columns[c]].astype(jnp.float32)
            ).astype(jnp.bfloat16)
            reduce(way, s, c).start()

        when((b < last - 1) & (b > target) if way else (b > 1) & (b < target), act)

    def serve(c):
        guest_copy(c).wait_recv() if c < 2 else None
        for s in range(last):
            target = jnp.where(b == 1, last - s, s)
            if c == 2:
                weight_copy(s).wait_recv()
            own = hard_sums[target, :, columns[c]].astype(jnp.float32)
            hard_sums[target, :, columns[c]] = (
                own + dot(guest_hard[s], guest[:, columns[c]], 0, 0)
            ).astype(jnp.bfloat16)
            if s < last - 1:
                when(b == 1, lambda: reduce(0, s, c).start())
                when(b == last - 1, lambda: reduce(1, s, c).start())

    when(host, lambda: serve(2))
    when(host, lambda: serve(1))
    for s in range(last):
        when(b == last, lambda: gather(0, last - 1 - s, s, 1).wait_recv())
        when(b == 0, lambda: gather(1, 1 + s, s, 1).wait_recv())

    for j in range(0, width, tile):
        query_dir[:, j:j + tile] = dot(
            grad_in[...], group[:, :, j:j + tile].reshape(ng * block, tile), 1, 0
        ) + dot(grad_hard[...], line[:, :, j:j + tile].reshape(nb * block, tile), 1, 0)

    def finish_queries(i, _):
        at = pl.ds(pl.multiple_of(i * ROWS, ROWS), ROWS)
        norm = query_norm[at, :]
        unit = queries[at, :].astype(jnp.float32) * norm
        direction = query_dir[at, :]
        inner = jnp.sum(unit * direction, axis=1, keepdims=True)
        query_out[at, :] = (norm * (direction - unit * inner)).astype(jnp.bfloat16)
        return _

    lax.fori_loop(0, rows // ROWS, finish_queries, 0)

    for c in (2, 1, 0):
        if c == 1:
            when(host, lambda: serve(0))
        for s in range(last - 1):
            add_and_pass(0, s, c)
            add_and_pass(1, s, c)
    for k in range(1, ng):
        back_copy(k).wait_recv()

    def finish_passages(at):
        total = hard_sums[b, at, :].astype(jnp.float32) + in_sums[g, at, :].astype(jnp.float32)
        for k in range(ng - 1):
            total += from_group[k, at, :].astype(jnp.float32)
        return total

    left_at = jnp.minimum(last - b, last - 2)
    right_at = jnp.minimum(b, last - 2)
    for c in range(PIECES):
        for way in (0, 1):
            for s in range(last - 1):
                target = s if way else last - s
                when(b == target, lambda: reduce(way, s, c).wait_recv())

    def finish(i, _):
        at = pl.ds(pl.multiple_of(i * ROWS, ROWS), ROWS)
        direction = finish_passages(at)
        direction += jnp.where(b > 1, from_left[left_at, at, :].astype(jnp.float32), 0.0)
        direction += jnp.where(b < last - 1, from_right[right_at, at, :].astype(jnp.float32), 0.0)
        norm = passage_norm[at, :]
        unit = passages[at, :].astype(jnp.float32) * norm
        inner = jnp.sum(unit * direction, axis=1, keepdims=True)
        passage_out[at, :] = (norm * (direction - unit * inner)).astype(jnp.bfloat16)
        return _

    lax.fori_loop(0, block // ROWS, finish, 0)

    for s in range(last):
        for c in range(2):
            when((b < last) & (b >= s), lambda: gather(0, b - s, s, c).wait_send())
            when((b > 0) & (b + s <= last), lambda: gather(1, b + s, s, c).wait_send())
        when(end, lambda: weight_copy(s).wait_send())
        when(host, lambda: share_copy(s).wait_send())
    for s in range(last - 1):
        for c in range(PIECES):
            when((b > 0) & (b < last - s), lambda: reduce(0, s, c).wait_send())
            when((b < last) & (b > s), lambda: reduce(1, s, c).wait_send())
    for c in range(PIECES):
        when(end, lambda: guest_copy(c).wait_send())
    for k in range(1, ng):
        group_copy(group.at[g], group.at[g], group_send, group_recv, k).wait_send()
        back_copy(k).wait_send()


def local_fused(queries, passages, hard_owners):
    rows, width = queries.shape
    block = passages.shape[0]
    nb, ng = lax.axis_size("batch"), lax.axis_size("grp")
    half, wide = jnp.bfloat16, jnp.float32
    vmem = pl.BlockSpec(memory_space=pltpu.VMEM)
    far = pl.BlockSpec(memory_space=pl.ANY)
    line_sems = pltpu.SemaphoreType.DMA((2, nb - 1, 2))
    sum_sems = pltpu.SemaphoreType.DMA((2, nb - 2, PIECES))
    pair_sems = pltpu.SemaphoreType.DMA((2,))
    guest_sems = pltpu.SemaphoreType.DMA((PIECES,))
    weight_sems = pltpu.SemaphoreType.DMA((nb - 1,))
    group_sems = pltpu.SemaphoreType.DMA((ng,))
    loss, query_grad, passage_grad = pl.pallas_call(
        functools.partial(fused_kernel, nb, ng),
        out_shape=(
            jax.ShapeDtypeStruct((rows,), wide),
            jax.ShapeDtypeStruct((rows, width), half),
            jax.ShapeDtypeStruct((block, width), half),
        ),
        in_specs=[far, far, vmem],
        out_specs=(vmem,) * 3,
        scratch_shapes=[
            pltpu.VMEM((rows, width), half),
            pltpu.VMEM((block, width), half),
            pltpu.VMEM((nb, block, width), half),
            pltpu.VMEM((ng, block, width), half),
            pltpu.VMEM((rows, width), half),
            pltpu.VMEM((rows, 1), wide),
            pltpu.VMEM((block, 1), wide),
            pltpu.VMEM((rows, ng * block), half),
            pltpu.VMEM((rows, nb * block), half),
            pltpu.VMEM((rows, width), wide),
            pltpu.VMEM((nb, block, width), half),
            pltpu.VMEM((nb - 2, block, width), half),
            pltpu.VMEM((nb - 2, block, width), half),
            pltpu.VMEM((ng, block, width), half),
            pltpu.VMEM((ng - 1, block, width), half),
            pltpu.VMEM((nb, rows, block), half),
            pltpu.VMEM((rows, width), half),
            pltpu.VMEM((nb - 1, rows, block), half),
            pltpu.VMEM((nb - 1, rows, block), half),
            pltpu.VMEM((nb - 1, rows, block), half),
            pltpu.VMEM((hard_owners.shape[1], rows, 1), wide),
            pltpu.VMEM((nb, rows, block), wide),
            pltpu.VMEM((rows, block), wide),
            pltpu.VMEM((rows, ng * block), wide),
            pltpu.VMEM((rows, 1), wide),
            pltpu.VMEM((rows, 1), wide),
            pair_sems, guest_sems, guest_sems, weight_sems, weight_sems, weight_sems, weight_sems,
            line_sems, line_sems, group_sems, group_sems,
            sum_sems, sum_sems, group_sems, group_sems,
        ],
        compiler_params=pltpu.CompilerParams(
            collective_id=0, has_side_effects=True, vmem_limit_bytes=56 * 1024 * 1024
        ),
        cost_estimate=pl.CostEstimate(
            flops=6 * rows * (nb + ng) * block * width,
            bytes_accessed=4 * (rows + block) * width,
            transcendentals=rows * (nb + ng) * block,
        ),
    )(queries, passages, hard_owners.T)
    return (loss, query_grad, passage_grad)


def local(queries, passages, hard_owners):
    nb = lax.axis_size("batch")
    if queries.shape[1] % 1024 == 0 and 4 <= nb <= 8 and 1 < lax.axis_size("grp") <= 8:
        return local_fused(queries, passages, hard_owners)
    if nb <= 8:
        return local_dense(queries, passages, hard_owners)
    return local_slots(queries, passages, hard_owners)


def solution(mesh):
    placed = (
        P(("parts", "batch", "grp"), None),
        P(("parts", "batch", "grp"), None),
        P(("parts", "batch", "grp"), None),
    )
    return jax.shard_map(
        local,
        mesh=mesh,
        in_specs=placed,
        out_specs=(
            P(("parts", "batch", "grp")),
            P(("parts", "batch", "grp"), None),
            P(("parts", "batch", "grp"), None),
        ),
        check_vma=False,
    )
```
